256 devices in a mesh: lev: 32 (over y, x, core), lon: 8 (over z).
Axes of the slice: x: 4, y: 4, z: 8, core: 2. Of those that a mesh axis runs over, the one named last changes fastest.
Arguments:
- levels_in: bfloat16 [128, 192, 96, 128], P('lev', None, 'lon'), may hold values from -6 to 6
- slab_levels: int32 [32], replicated, may hold values from 1 to 4, 64 in all
- shifts: int32 [32], replicated, may hold values from 0 to 11
- gain_col: float32 [128], replicated, may hold values from 0.1 to 1.9
- w_col_qkv: bfloat16 [128, 384], replicated
- w_col_out: bfloat16 [128, 128], replicated, may hold values from -0.5 to 0.5
- gain_win: float32 [128], replicated, may hold values from 0.1 to 1.9
- w_win_qkv: bfloat16 [128, 384], replicated
- w_win_out: bfloat16 [128, 128], replicated, may hold values from -0.5 to 0.5
- gain_mlp: float32 [128], replicated, may hold values from 0.1 to 1.9
- w_up: bfloat16 [128, 512], replicated, may hold values from -0.5 to 0.5
- w_down: bfloat16 [512, 128], replicated, may hold values from -0.25 to 0.25
Outputs:
- levels_out: bfloat16 [128, 192, 96, 128], P('lev', None, 'lon')
The draws below stay inside these ranges and needn't reach their ends.
All inputs are finite; a program needn't handle non-finite values.
Results may differ from the reference program's by a relative error of at most 0.0095.
Values may be sent and summed in bfloat16 or wider, within the bound.
A program may use at most 128 MiB of HBM per device.

```python
import math
import jax
import jax.numpy as jnp
import numpy as np
from jax import lax

C = 128
HEADS = 4
FFN = 512
WLEV = 2
WLAT = 6
WLON = 12
LEV = 64
LCAP = 4
H = 192
W = 96
N_LEV = 32


def qkv_draw(key, boost):
    key_query, key_other, key_value = jax.random.split(key, 3)
    scale = C ** (-0.5)
    head_strength = 1.0 + boost * jnp.arange(HEADS, dtype=jnp.float32) / max(HEADS - 1, 1)
    column_strength = jnp.repeat(head_strength, C // HEADS)
    query_part = jax.random.normal(key_query, (C, C), jnp.float32) * scale * column_strength[None, :]
    other_part = jax.random.normal(key_other, (C, C), jnp.float32) * scale
    key_part = other_part
    value_part = jax.random.normal(key_value, (C, C), jnp.float32) * scale
    return jnp.concatenate([query_part, key_part, value_part], 1).astype(jnp.bfloat16)


def draw_w_col_qkv(key, part):
    key = jax.random.fold_in(key, 11)
    return qkv_draw(key, 0.0)


def draw_w_win_qkv(key, part):
    key = jax.random.fold_in(key, 23)
    return qkv_draw(key, 0.0)


def with_ends(result, key, least, high):
    place = [jax.random.randint(jax.random.fold_in(key, axis), (), 0, length) for axis, length in enumerate(result.shape)]
    longest = result.shape.index(max(result.shape))
    next_to = place[:longest] + [(place[longest] + 1) % result.shape[longest]] + place[longest + 1:]
    return result.at[tuple(place)].set(least).at[tuple(next_to)].set(high)


def block_levels(rng, dims, pieces, low, largest):
    level, own = 1.0, jax.random.fold_in(rng, 6)
    for axis_at, blocks in pieces:
        steps = jnp.exp(jax.random.uniform(jax.random.fold_in(own, axis_at), (blocks,), jnp.float32, low / len(pieces), largest / len(pieces)))
        level = level * jnp.repeat(steps, dims[axis_at] // blocks).reshape([-1 if axis == axis_at else 1 for axis in range(len(dims))])
    return level


def split_up(number_of, total, bound, lean):
    portions = [(1 << 20) // math.isqrt(standing ** lean) + 1 for standing in range(2, number_of + 1)]
    surplus, given = total - bound - (number_of - 1), [1] * (number_of - 1)
    while surplus > 0:
        movable = [i for i in range(number_of - 1) if given[i] < bound]
        pool, budget = sum([portions[i] for i in movable]), surplus
        for i in movable:
            addition = min(bound - given[i], max(1, budget * portions[i] // pool), surplus)
            given[i] = given[i] + addition
            surplus = surplus - addition
    return np.array([bound] + given)


def uneven(key, count, total, most, slope):
    if count == 2:
        one = jax.random.randint(key, (), max(1, total - most), min(most, total - 1) + 1)
        return jnp.stack([one, total - one])
    lengths = jnp.asarray(split_up(count, total, most, slope), jnp.int32)
    couples = (count - 1) // 2
    donor, receiver = lengths[1:1 + 2 * couples:2], lengths[2:2 + 2 * couples:2]
    margin = jnp.minimum(donor - 1, most - receiver)
    shifted = jax.random.randint(jax.random.fold_in(key, 1), (couples,), 0, 1 << 20) % (margin + 1)
    lengths = lengths.at[1:1 + 2 * couples:2].set(donor - shifted).at[2:2 + 2 * couples:2].set(receiver + shifted)
    return lengths[jax.random.permutation(jax.random.fold_in(key, 2), count)]


def normal_values(rng, shape, scale, reach, pieces=(), kind=jnp.bfloat16):
    drawn = scale * jax.random.normal(rng, shape, jnp.float32)
    if pieces:
        drawn = drawn * block_levels(rng, shape, pieces, -0.22, 0.18)
    return jnp.clip(drawn, -reach, reach).astype(kind)


def setup_inputs(seed: int = 0) -> dict:
    key_of = jax.random.split(jax.random.key(seed), 13)
    return {
        "levels_in": normal_values(key_of[0], (N_LEV * LCAP, H, W, C), 1.0, 6.0, ((0, 32), (2, 8))),
        "slab_levels": uneven(key_of[1], N_LEV, LEV, LCAP, 2).astype(jnp.int32),
        "shifts": with_ends(jax.random.randint(key_of[2], (LEV // WLEV,), 0, WLON), jax.random.fold_in(key_of[2], 1), 0, WLON - 1).astype(jnp.int32),
        "gain_col": jnp.clip(1.0 + 0.18 * jax.random.normal(key_of[3], (C,), jnp.float32), 0.1, 1.9),
        "w_col_qkv": draw_w_col_qkv(jax.random.fold_in(key_of[12], 71), 0),
        "w_col_out": normal_values(key_of[5], (C, C), C ** -0.5, 0.5),
        "gain_win": jnp.clip(1.0 + 0.18 * jax.random.normal(key_of[6], (C,), jnp.float32), 0.1, 1.9),
        "w_win_qkv": draw_w_win_qkv(jax.random.fold_in(key_of[12], 71), 0),
        "w_win_out": normal_values(key_of[8], (C, C), C ** -0.5, 0.5),
        "gain_mlp": jnp.clip(1.0 + 0.18 * jax.random.normal(key_of[9], (C,), jnp.float32), 0.1, 1.9),
        "w_up": normal_values(key_of[10], (C, FFN), C ** -0.5, 0.5),
        "w_down": normal_values(key_of[11], (FFN, C), FFN ** -0.5, 0.25),
    }


EPS = 1e-05

def layer_norm(features, gain_vec):
    features = features.astype(jnp.float32)
    centred = features - lax.optimization_barrier(jnp.mean(features, -1, keepdims=True))
    spread = lax.optimization_barrier(jnp.mean(centred * centred, -1, keepdims=True))
    return (centred * lax.rsqrt(spread + EPS) * gain_vec).astype(jnp.bfloat16)

def attend(normed, w_qkv):
    batch_size, seq_len, feature_dim = normed.shape
    head_size = feature_dim // HEADS
    packed = jnp.einsum('bsc,cf->bsf', normed.astype(jnp.float32), w_qkv.astype(jnp.float32), precision=lax.Precision.HIGHEST).astype(jnp.bfloat16)
    packed = lax.optimization_barrier(packed)
    packed = packed.astype(jnp.float32).reshape(batch_size, seq_len, 3, HEADS, head_size)
    scores = jnp.einsum('bqhd,bkhd->bhqk', packed[:, :, 0], packed[:, :, 1], precision=lax.Precision.HIGHEST) / math.sqrt(head_size)
    weights = jax.nn.softmax(scores, -1).astype(jnp.bfloat16)
    weights = lax.optimization_barrier(weights)
    attended = jnp.einsum('bhqk,bkhd->bqhd', weights.astype(jnp.float32), packed[:, :, 2], precision=lax.Precision.HIGHEST)
    return attended.reshape(batch_size, seq_len, feature_dim).astype(jnp.bfloat16)

def project(rows, weight):
    flat = rows.reshape(-1, rows.shape[-1])
    return jnp.dot(flat, weight, preferred_element_type=jnp.float32)

def reference(levels_in, slab_levels, shifts, gain_col, w_col_qkv, w_col_out, gain_win, w_win_qkv, w_win_out, gain_mlp, w_up, w_down):
    counts = slab_levels.astype(jnp.int32)
    slab_ends = jnp.cumsum(counts).astype(jnp.int32)
    starts = (slab_ends - counts).astype(jnp.int32)
    level_ids = jnp.arange(LEV, dtype=jnp.int32)
    owner_dev = lax.optimization_barrier(jnp.sum((slab_ends[None, :] <= level_ids[:, None]).astype(jnp.int32), 1)).astype(jnp.int32)
    source_rows = (owner_dev * LCAP + level_ids - starts[owner_dev]).astype(jnp.int32)
    columns = jnp.take(levels_in, source_rows, axis=0)
    band_count = LEV // WLEV
    win_count = W // WLON
    blocks = columns.reshape(LEV, H // WLAT, WLAT, W, C).transpose(1, 0, 2, 3, 4)

    def one_block(block_rows):
        normed = layer_norm(block_rows, gain_col).reshape(LEV, WLAT * W, C).transpose(1, 0, 2)
        attended = attend(normed, w_col_qkv).transpose(1, 0, 2)
        after_column = block_rows.reshape(-1, C).astype(jnp.float32) + project(attended, w_col_out)
        normed = layer_norm(after_column, gain_win).reshape(band_count, WLEV, WLAT, W, C)
        rolled = jax.vmap(lambda band_rows, offset: jnp.roll(band_rows, -offset, axis=2))(normed, shifts)
        windows = rolled.reshape(band_count, WLEV, WLAT, win_count, WLON, C).transpose(0, 3, 1, 2, 4, 5)
        windows = windows.reshape(band_count * win_count, WLEV * WLAT * WLON, C)
        attended = attend(windows, w_win_qkv).reshape(band_count, win_count, WLEV, WLAT, WLON, C)
        attended = attended.transpose(0, 2, 3, 1, 4, 5).reshape(band_count, WLEV, WLAT, W, C)
        attended = jax.vmap(lambda band_rows, offset: jnp.roll(band_rows, offset, axis=2))(attended, shifts)
        after_window = after_column + project(attended, w_win_out)
        normed = layer_norm(after_window, gain_mlp)
        hidden = jax.nn.gelu(project(normed, w_up), approximate=True).astype(jnp.bfloat16)
        block_out = (after_window + project(hidden, w_down)).astype(jnp.bfloat16)
        return block_out.reshape(LEV, WLAT, W, C)
    results = lax.map(one_block, blocks)
    block_out = results.transpose(1, 0, 2, 3, 4).reshape(LEV, H, W, C)
    slot_ids = jnp.arange(N_LEV * LCAP, dtype=jnp.int32)
    slot_owner = (slot_ids // LCAP).astype(jnp.int32)
    slot_offset = (slot_ids % LCAP).astype(jnp.int32)
    in_slab = slot_offset < counts[slot_owner]
    target = jnp.minimum(starts[slot_owner] + slot_offset, LEV - 1).astype(jnp.int32)
    picked = jnp.take(block_out, target, axis=0)
    return jnp.where(in_slab[:, None, None, None], picked, jnp.zeros_like(picked)).astype(jnp.bfloat16)
```

```python
import functools
import math

import jax
import jax.numpy as jnp
from jax import lax
from jax.experimental import pallas as pl
from jax.experimental.pallas import tpu as pltpu
from jax.sharding import PartitionSpec as P

HEADS = 4
EPS = 1e-05
MESH = pl.DeviceIdType.MESH
F32 = jnp.float32
BF16 = jnp.bfloat16

SLOTS = 4
LON = 12
LAT = 6
HALF = LON // 2
LEVD = 32
LEV = 64
LATS = LAT * LEVD
C = 128
COLS = HALF * LAT
ROWS_IN = SLOTS * LON
ROWS_OUT = SLOTS * COLS
HROWS = LEV * COLS
PAIR = 4 * COLS
PAIRS = LEV // 4
GROUPS = 4
GROUP = PAIRS // GROUPS
HCOL = HALF * LEV
SCALE = math.log2(math.e) / math.sqrt(C // HEADS)


def norm(v, gain):
    centred = v - jnp.mean(v, -1, keepdims=True)
    spread = jnp.mean(centred * centred, -1, keepdims=True)
    return (centred * lax.rsqrt(spread + EPS) * gain).astype(BF16)


def dot(a, b):
    return jnp.dot(a, b, preferred_element_type=F32)


def dot_nt(a, b):
    return lax.dot_general(a, b, (((1,), (1,)), ((), ())), preferred_element_type=F32)


def head_masks(rows):
    lane = lax.broadcasted_iota(jnp.int32, (rows, C), 1)
    return [(lane // (C // HEADS)) == h for h in range(HEADS)]


def attend(q, k, v, masks):
    n = q.shape[0]
    value = jnp.concatenate([v, jnp.ones((n, C), BF16)], 1)
    total = None
    for h in range(HEADS):
        scores = dot_nt(jnp.where(masks[h], q, jnp.zeros_like(q)), k)
        top = jnp.max(scores, -1, keepdims=True)
        probs = jnp.exp2((scores - top) * SCALE).astype(BF16)
        both = dot(probs, value)
        part = both[:, :C] / both[:, C:]
        total = part if total is None else jnp.where(masks[h], part, total)
    return total


def plane_target(me, step):
    core, x, y = lax.rem(me, 2), lax.rem(me // 2, 4), me // 8
    dc, dx, dy = lax.rem(step, 2), lax.rem(step // 2, 4), step // 8
    return (lax.rem(y + dy, 4) * 4 + lax.rem(x + dx, 4)) * 2 + lax.rem(core + dc, 2)


def kernel(
    counts_ref, shifts_ref, x_ref, gcol_ref, wcq_ref, wco_ref, gwin_ref, wwq_ref, wwo_ref,
    gmlp_ref, wup_ref, wdn_ref, out_ref,
    rowoff, starts, big, sendbuf, recv, r32, xl, srow, after, hsend, hrecv, wtok, attd, back,
    blk, msg, got,
    in_send, in_recv, h_send, h_recv, b_send, b_recv, o_send, o_recv,
):
    me = lax.axis_index("lev")
    z = lax.axis_index("lon")
    east = lax.rem(z + 1, 8)
    west = lax.rem(z + 7, 8)

    barrier = pltpu.get_barrier_semaphore()

    def greet(step, _):
        pl.semaphore_signal(barrier, inc=1, device_id={"lev": plane_target(me, step)}, device_id_type=MESH)
        return 0

    lax.fori_loop(1, LEVD, greet, 0)
    for side in (east, west):
        pl.semaphore_signal(barrier, inc=1, device_id={"lon": side}, device_id_type=MESH)

    def widen(n, _):
        big[pl.ds(pl.multiple_of(n * LATS, LATS), LATS), :] = x_ref[n].astype(F32)
        return 0

    lax.fori_loop(0, ROWS_IN, widen, 0)
    pl.semaphore_wait(barrier, LEVD - 1 + 2)

    def in_copy(i, dest):
        return pltpu.make_async_remote_copy(
            src_ref=sendbuf.at[i, dest], dst_ref=recv.at[i, me],
            send_sem=in_send.at[i], recv_sem=in_recv.at[i],
            device_id={"lev": dest}, device_id_type=MESH,
        )

    def send_chunk(i, _):
        def one(step, _):
            dest = plane_target(me, LEVD - step)
            sendbuf[i, dest] = big[pl.ds(dest * LAT + i, ROWS_IN, stride=LATS), :].astype(BF16)
            in_copy(i, dest).start()
            return 0

        lax.fori_loop(1, LEVD, one, 0)
        recv[i, me] = big[pl.ds(me * LAT + i, ROWS_IN, stride=LATS), :].astype(BF16)
        return 0

    lax.fori_loop(0, LAT, send_chunk, 0)

    def place(level, carry):
        slab, slot = carry
        rowoff[level] = jnp.minimum(slab, LEVD - 1) * ROWS_IN + jnp.minimum(slot, SLOTS - 1) * LON
        more = slot + 1
        ends = more >= counts_ref[jnp.minimum(slab, LEVD - 1)]
        return jnp.where(ends, slab + 1, slab), jnp.where(ends, 0, more)

    lax.fori_loop(0, LEV, place, (jnp.int32(0), jnp.int32(0)))

    def begin(slab, start):
        starts[slab] = jnp.minimum(start, LEV - 1)
        return start + counts_ref[slab]

    lax.fori_loop(0, LEVD, begin, jnp.int32(0))

    def shift_rows(level, _):
        srow[pl.ds(level, 1), :] = jnp.full((1, C), shifts_ref[level // 2], jnp.int32)
        return 0

    lax.fori_loop(0, LEV, shift_rows, 0)

    def halo_copy(i, half, side):
        return pltpu.make_async_remote_copy(
            src_ref=hsend.at[i, half], dst_ref=hrecv.at[i, half],
            send_sem=h_send.at[i, half], recv_sem=h_recv.at[i, half],
            device_id={"lon": side}, device_id_type=MESH,
        )

    masks64 = head_masks(LEV)

    def column_chunk(i, _):
        pltpu.make_async_copy(
            recv.at[i, pl.ds(0, LEVD - 1)], recv.at[i, pl.ds(0, LEVD - 1)], in_recv.at[i]
        ).wait()

        def widen_in(d, _):
            r32[pl.ds(pl.multiple_of(d * ROWS_IN, ROWS_IN), ROWS_IN), :] = recv[i, d].astype(F32)
            return 0

        lax.fori_loop(0, LEVD, widen_in, 0)

        def pick(level, _):
            xl[pl.ds(pl.multiple_of(level * 16, 16), 16), :] = r32[pl.ds(rowoff[level], 16), :]
            return 0

        lax.fori_loop(0, LEV, pick, 0, unroll=8)

        for half in range(2):
            for first in range(0, HALF, 3):
                lons = [half * HALF + first + n for n in range(3)]
                cols = jnp.concatenate([xl[pl.ds(lon, LEV, stride=16), :] for lon in lons], 0)
                packed = dot(norm(cols, gcol_ref[...]), wcq_ref[...]).astype(BF16)
                parts = []
                for n in range(3):
                    one = packed[n * LEV:(n + 1) * LEV]
                    parts.append(attend(one[:, :C], one[:, C:2 * C], one[:, 2 * C:], masks64))
                attended = jnp.concatenate(parts, 0).astype(BF16)
                done = cols + dot(attended, wco_ref[...])
                normed = norm(done, gwin_ref[...])
                for n in range(3):
                    at = half * HROWS + i * HALF + first + n
                    after[pl.ds(at, LEV, stride=COLS), :] = done[n * LEV:(n + 1) * LEV]
                    hsend[i, half, pl.ds((first + n) * LEV, LEV), :] = normed[n * LEV:(n + 1) * LEV]
            halo_copy(i, half, west if half == 0 else east).start()
        return 0

    def merge_chunk(i, _):
        for half in range(2):
            halo_copy(i, half, west if half == 0 else east).wait_recv()
            for n in range(HALF):
                lon = half * HALF + n
                shift = srow[...]
                own = (lon >= shift) == (shift <= HALF)
                mine = hsend[i, half, pl.ds(n * LEV, LEV), :].astype(F32)
                other = hrecv[i, half, pl.ds(n * LEV, LEV), :].astype(F32)
                at = half * HROWS + i * HALF + n
                wtok[pl.ds(at, LEV, stride=COLS), :] = jnp.where(own, mine, other)
        return 0

    def both_chunks(i, _):
        column_chunk(i, 0)
        merge_chunk(i - 1, 0)
        return 0

    column_chunk(0, 0)
    lax.fori_loop(1, LAT, both_chunks, 0)
    merge_chunk(LAT - 1, 0)

    masks144 = head_masks(PAIR)

    def back_copy(g, half, side):
        part = pl.ds(pl.multiple_of(g * (GROUP * PAIR), GROUP * PAIR), GROUP * PAIR)
        return pltpu.make_async_remote_copy(
            src_ref=attd.at[half, part], dst_ref=back.at[half, part],
            send_sem=b_send.at[half, g], recv_sem=b_recv.at[half, g],
            device_id={"lon": side}, device_id_type=MESH,
        )

    def window_pair(p, _):
        at = pl.multiple_of(p * PAIR, PAIR)
        quarters = []
        for band in range(2):
            for half in range(2):
                quarters.append(wtok[pl.ds(at + half * HROWS + band * (PAIR // 2), PAIR // 2), :])
        tokens = jnp.concatenate(quarters, 0).astype(BF16)
        packed = dot(tokens, wwq_ref[...]).astype(BF16)
        bands = []
        for band in range(2):
            one = packed[band * PAIR:(band + 1) * PAIR]
            bands.append(attend(one[:, :C], one[:, C:2 * C], one[:, 2 * C:], masks144))
        for half in range(2):
            rows = slice(half * (PAIR // 2), (half + 1) * (PAIR // 2))
            attd[half, pl.ds(at, PAIR), :] = jnp.concatenate([b[rows] for b in bands], 0).astype(BF16)
        return 0

    def window_group(g, _):
        lax.fori_loop(g * GROUP, (g + 1) * GROUP, window_pair, 0)
        back_copy(g, 0, east).start()
        back_copy(g, 1, west).start()
        return 0

    lax.fori_loop(0, GROUPS, window_group, 0)

    def out_copy(half, dest):
        return pltpu.make_async_remote_copy(
            src_ref=msg.at[half, dest], dst_ref=got.at[half, me],
            send_sem=o_send.at[half], recv_sem=o_recv.at[half],
            device_id={"lev": dest}, device_id_type=MESH,
        )

    row = lax.broadcasted_iota(jnp.int32, (PAIR, C), 0)
    for half in range(2):
        lon_of_row = lax.rem(row, HALF) + half * HALF

        def feed_pair(p, _):
            at = pl.multiple_of(p * PAIR, PAIR)
            shift = jnp.where(row < PAIR // 2, shifts_ref[2 * p], shifts_ref[2 * p + 1])
            own = (lon_of_row >= shift) == (shift <= HALF)
            attended = jnp.where(
                own, attd[half, pl.ds(at, PAIR), :].astype(F32), back[half, pl.ds(at, PAIR), :].astype(F32)
            ).astype(BF16)
            stay = after[pl.ds(at + half * HROWS, PAIR), :] + dot(attended, wwo_ref[...])
            hidden = jax.nn.gelu(dot(norm(stay, gmlp_ref[...]), wup_ref[...]), approximate=True)
            blk[half, pl.ds(at, PAIR), :] = stay + dot(hidden.astype(BF16), wdn_ref[...])
            return 0

        def feed_group(g, _):
            back_copy(g, half, east if half == 0 else west).wait_recv()
            lax.fori_loop(g * GROUP, (g + 1) * GROUP, feed_pair, 0)
            return 0

        blk[half, pl.ds(HROWS, PAIR), :] = jnp.zeros((PAIR, C), F32)
        lax.fori_loop(0, GROUPS, feed_group, 0)

        def block_for(dest):
            rows = blk[half, pl.ds(starts[dest] * COLS, ROWS_OUT), :]
            return jnp.where(row < counts_ref[dest] * COLS, rows, 0.0).astype(BF16)

        def send_out(step, _):
            dest = plane_target(me, LEVD - step)
            msg[half, dest] = block_for(dest)
            out_copy(half, dest).start()
            return 0

        lax.fori_loop(1, LEVD, send_out, 0)
        got[half, me] = block_for(me)

    for half in range(2):
        pltpu.make_async_copy(
            got.at[half, pl.ds(0, LEVD - 1)], got.at[half, pl.ds(0, LEVD - 1)], o_recv.at[half]
        ).wait()

        def widen_out(e, _):
            big[pl.ds(pl.multiple_of(e * ROWS_OUT, ROWS_OUT), ROWS_OUT), :] = got[half, e].astype(F32)
            return 0

        lax.fori_loop(0, LEVD, widen_out, 0)

        def unpack(n, _):
            slot, lon = n // HALF, lax.rem(n, HALF)
            for i in range(LAT):
                r32[pl.ds(i, LEVD, stride=LAT), :] = big[
                    pl.ds(slot * COLS + i * HALF + lon, LEVD, stride=ROWS_OUT), :
                ]
            out_ref[slot * LON + half * HALF + lon] = r32[pl.ds(0, LATS), :].astype(BF16)
            return 0

        lax.fori_loop(0, SLOTS * HALF, unpack, 0)

    for i in range(LAT):
        pltpu.make_async_copy(
            sendbuf.at[i, pl.ds(0, LEVD - 1)], sendbuf.at[i, pl.ds(0, LEVD - 1)], in_send.at[i]
        ).wait()
        halo_copy(i, 0, west).wait_send()
        halo_copy(i, 1, east).wait_send()
    for g in range(GROUPS):
        back_copy(g, 0, east).wait_send()
        back_copy(g, 1, west).wait_send()
    for half in range(2):
        pltpu.make_async_copy(
            msg.at[half, pl.ds(0, LEVD - 1)], msg.at[half, pl.ds(0, LEVD - 1)], o_send.at[half]
        ).wait()


def per_device(
    levels_in, slab_levels, shifts, gain_col, w_col_qkv, w_col_out, gain_win, w_win_qkv, w_win_out,
    gain_mlp, w_up, w_down,
):
    x = levels_in.transpose(0, 2, 1, 3).reshape(ROWS_IN, LATS, C)
    smem = pl.BlockSpec(memory_space=pltpu.SMEM)
    vmem = pl.BlockSpec(memory_space=pltpu.VMEM)
    dma = pltpu.SemaphoreType.DMA
    out = pl.pallas_call(
        kernel,
        out_shape=jax.ShapeDtypeStruct((ROWS_IN, LATS, C), BF16),
        in_specs=[smem, smem] + [vmem] * 10,
        out_specs=vmem,
        scratch_shapes=[
            pltpu.SMEM((LEV,), jnp.int32),
            pltpu.SMEM((LEVD,), jnp.int32),
            pltpu.VMEM((ROWS_IN * LATS, C), F32),
            pltpu.VMEM((LAT, LEVD, ROWS_IN, C), BF16),
            pltpu.VMEM((LAT, LEVD, ROWS_IN, C), BF16),
            pltpu.VMEM((LEVD * ROWS_IN + 8, C), F32),
            pltpu.VMEM((LEV * 16, C), F32),
            pltpu.VMEM((LEV, C), jnp.int32),
            pltpu.VMEM((2 * HROWS, C), F32),
            pltpu.VMEM((LAT, 2, HCOL, C), BF16),
            pltpu.VMEM((LAT, 2, HCOL, C), BF16),
            pltpu.VMEM((2 * HROWS, C), F32),
            pltpu.VMEM((2, HROWS, C), BF16),
            pltpu.VMEM((2, HROWS, C), BF16),
            pltpu.VMEM((2, HROWS + PAIR, C), F32),
            pltpu.VMEM((2, LEVD, ROWS_OUT, C), BF16),
            pltpu.VMEM((2, LEVD, ROWS_OUT, C), BF16),
            dma((LAT,)), dma((LAT,)),
            dma((LAT, 2)), dma((LAT, 2)),
            dma((2, GROUPS)), dma((2, GROUPS)),
            dma((2,)), dma((2,)),
        ],
        compiler_params=pltpu.CompilerParams(
            collective_id=0, has_side_effects=True, vmem_limit_bytes=56 * 1024 * 1024
        ),
    )(
        slab_levels, shifts, x, gain_col.reshape(1, C), w_col_qkv, w_col_out, gain_win.reshape(1, C),
        w_win_qkv, w_win_out, gain_mlp.reshape(1, C), w_up, w_down,
    )
    return out.reshape(SLOTS, LON, LATS, C).transpose(0, 2, 1, 3)


def solution(mesh):
    placed = (P("lev", None, "lon", None),) + (P(),) * 11
    return jax.shard_map(
        per_device,
        mesh=mesh,
        in_specs=placed,
        out_specs=P("lev", None, "lon", None),
        check_vma=False,
    )
```

```python
import functools
import math

import jax
import jax.numpy as jnp
from jax import lax
from jax.experimental import pallas as pl
from jax.experimental.pallas import tpu as pltpu
from jax.sharding import PartitionSpec as P

HEADS = 4
EPS = 1e-05
MESH = pl.DeviceIdType.MESH
F32 = jnp.float32
BF16 = jnp.bfloat16

SLOTS = 4
LON = 12
LAT = 6
HALF = LON // 2
LEVD = 32
LEV = 64
LATS = LAT * LEVD
C = 128
COLS = HALF * LAT
ROWS_IN = SLOTS * LON
ROWS_OUT = SLOTS * COLS
HROWS = LEV * COLS
PAIR = 4 * COLS
PAIRS = LEV // 4
GROUPS = 4
GROUP = PAIRS // GROUPS
HCOL = HALF * LEV
FEED = 4
WIN = 4
COLG = 6
GELU_A = math.sqrt(2.0 / math.pi)
GELU_B = GELU_A * 0.044715
SCALE = math.log2(math.e) / math.sqrt(C // HEADS)


def norm(v, gain):
    centred = v - jnp.mean(v, -1, keepdims=True)
    spread = jnp.mean(centred * centred, -1, keepdims=True)
    return (centred * lax.rsqrt(spread + EPS) * gain).astype(BF16)


def dot(a, b):
    return jnp.dot(a, b, preferred_element_type=F32)


def dot_nt(a, b):
    return lax.dot_general(a, b, (((1,), (1,)), ((), ())), preferred_element_type=F32)


def head_masks(rows):
    lane = lax.broadcasted_iota(jnp.int32, (rows, C), 1)
    return [(lane // (C // HEADS)) == h for h in range(HEADS)]


def attend(q, k, v, masks):
    n = q.shape[0]
    value = jnp.concatenate([v, jnp.ones((n, C), BF16)], 1)
    over, under = None, None
    for h in range(HEADS):
        scores = dot_nt(jnp.where(masks[h], q, jnp.zeros_like(q)), k)
        top = jnp.max(scores, -1, keepdims=True)
        probs = jnp.exp2((scores - top) * SCALE).astype(BF16)
        both = dot(probs, value)
        over = both[:, :C] if h == 0 else jnp.where(masks[h], both[:, :C], over)
        under = both[:, C:] if h == 0 else jnp.where(masks[h], both[:, C:], under)
    return over / under


def gelu(v):
    inner = v * (GELU_A + GELU_B * (v * v))
    half = 0.5 * v
    return half * jnp.tanh(inner) + half


def plane_target(me, step):
    core, x, y = lax.rem(me, 2), lax.rem(me // 2, 4), me // 8
    dc, dx, dy = lax.rem(step, 2), lax.rem(step // 2, 4), step // 8
    return (lax.rem(y + dy, 4) * 4 + lax.rem(x + dx, 4)) * 2 + lax.rem(core + dc, 2)


def kernel(
    counts_ref, shifts_ref, x_ref, gcol_ref, wcq_ref, wco_ref, gwin_ref, wwq_ref, wwo_ref,
    gmlp_ref, wup_ref, wdn_ref, out_ref,
    rowoff, starts, big, sendbuf, recv, r32, xl, srow, after, hsend, hrecv, wtok, attd, back,
    mask, blk, msg, got,
    in_send, in_recv, h_send, h_recv, b_send, b_recv, o_send, o_recv,
):
    me = lax.axis_index("lev")
    z = lax.axis_index("lon")
    east = lax.rem(z + 1, 8)
    west = lax.rem(z + 7, 8)

    barrier = pltpu.get_barrier_semaphore()

    def greet(step, _):
        pl.semaphore_signal(barrier, inc=1, device_id={"lev": plane_target(me, step)}, device_id_type=MESH)
        return 0

    lax.fori_loop(1, LEVD, greet, 0)
    for side in (east, west):
        pl.semaphore_signal(barrier, inc=1, device_id={"lon": side}, device_id_type=MESH)

    def widen(n, _):
        big[pl.ds(pl.multiple_of(n * LATS, LATS), LATS), :] = x_ref[n].astype(F32)
        return 0

    lax.fori_loop(0, ROWS_IN, widen, 0)
    pl.semaphore_wait(barrier, LEVD - 1 + 2)

    def in_copy(i, dest):
        return pltpu.make_async_remote_copy(
            src_ref=sendbuf.at[i, dest], dst_ref=recv.at[i, me],
            send_sem=in_send.at[i], recv_sem=in_recv.at[i],
            device_id={"lev": dest}, device_id_type=MESH,
        )

    def send_chunk(i, _):
        def one(step, _):
            dest = plane_target(me, LEVD - step)
            sendbuf[i, dest] = big[pl.ds(dest * LAT + i, ROWS_IN, stride=LATS), :].astype(BF16)
            in_copy(i, dest).start()
            return 0

        lax.fori_loop(1, LEVD, one, 0)
        recv[i, me] = big[pl.ds(me * LAT + i, ROWS_IN, stride=LATS), :].astype(BF16)
        return 0

    lax.fori_loop(0, LAT, send_chunk, 0)

    def place(level, carry):
        slab, slot = carry
        rowoff[level] = jnp.minimum(slab, LEVD - 1) * ROWS_IN + jnp.minimum(slot, SLOTS - 1) * LON
        more = slot + 1
        ends = more >= counts_ref[jnp.minimum(slab, LEVD - 1)]
        return jnp.where(ends, slab + 1, slab), jnp.where(ends, 0, more)

    lax.fori_loop(0, LEV, place, (jnp.int32(0), jnp.int32(0)))

    def begin(slab, start):
        starts[slab] = jnp.minimum(start, LEV - 1)
        return start + counts_ref[slab]

    lax.fori_loop(0, LEVD, begin, jnp.int32(0))

    def shift_rows(level, _):
        srow[pl.ds(level, 1), :] = jnp.full((1, C), shifts_ref[level // 2], jnp.int32)
        return 0

    lax.fori_loop(0, LEV, shift_rows, 0)

    row = lax.broadcasted_iota(jnp.int32, (PAIR, C), 0)

    def own_rows(p, _):
        shift = jnp.where(row < PAIR // 2, shifts_ref[2 * p], shifts_ref[2 * p + 1])
        for half in range(2):
            own = (lax.rem(row, HALF) + half * HALF >= shift) == (shift <= HALF)
            mask[half, pl.ds(pl.multiple_of(p * PAIR, PAIR), PAIR), :] = own.astype(jnp.int32)
        return 0

    lax.fori_loop(0, PAIRS, own_rows, 0)

    def halo_copy(i, half, side):
        return pltpu.make_async_remote_copy(
            src_ref=hsend.at[i, half], dst_ref=hrecv.at[i, half],
            send_sem=h_send.at[i, half], recv_sem=h_recv.at[i, half],
            device_id={"lon": side}, device_id_type=MESH,
        )

    masks64 = head_masks(LEV)

    def column_chunk(i, _):
        pltpu.make_async_copy(
            recv.at[i, pl.ds(0, LEVD - 1)], recv.at[i, pl.ds(0, LEVD - 1)], in_recv.at[i]
        ).wait()

        def widen_in(d, _):
            r32[pl.ds(pl.multiple_of(d * ROWS_IN, ROWS_IN), ROWS_IN), :] = recv[i, d].astype(F32)
            return 0

        lax.fori_loop(0, LEVD, widen_in, 0)

        def pick(level, _):
            xl[pl.ds(pl.multiple_of(level * 16, 16), 16), :] = r32[pl.ds(rowoff[level], 16), :]
            return 0

        lax.fori_loop(0, LEV, pick, 0, unroll=8)

        for half in range(2):
            for first in range(0, HALF, COLG):
                lons = [half * HALF + first + n for n in range(COLG)]
                cols = jnp.concatenate([xl[pl.ds(lon, LEV, stride=16), :] for lon in lons], 0)
                packed = dot(norm(cols, gcol_ref[...]), wcq_ref[...]).astype(BF16)
                parts = []
                for n in range(COLG):
                    one = packed[n * LEV:(n + 1) * LEV]
                    parts.append(attend(one[:, :C], one[:, C:2 * C], one[:, 2 * C:], masks64))
                attended = jnp.concatenate(parts, 0).astype(BF16)
                done = cols + dot(attended, wco_ref[...])
                normed = norm(done, gwin_ref[...])
                for n in range(COLG):
                    at = half * HROWS + i * HALF + first + n
                    after[pl.ds(at, LEV, stride=COLS), :] = done[n * LEV:(n + 1) * LEV]
                    hsend[i, half, pl.ds((first + n) * LEV, LEV), :] = normed[n * LEV:(n + 1) * LEV]
            halo_copy(i, half, west if half == 0 else east).start()
        return 0

    def merge_chunk(i, _):
        for half in range(2):
            halo_copy(i, half, west if half == 0 else east).wait_recv()
            for n in range(HALF):
                lon = half * HALF + n
                shift = srow[...]
                own = (lon >= shift) == (shift <= HALF)
                mine = hsend[i, half, pl.ds(n * LEV, LEV), :].astype(F32)
                other = hrecv[i, half, pl.ds(n * LEV, LEV), :].astype(F32)
                at = half * HROWS + i * HALF + n
                wtok[pl.ds(at, LEV, stride=COLS), :] = jnp.where(own, mine, other)
        return 0

    def both_chunks(i, _):
        column_chunk(i, 0)
        merge_chunk(i - 1, 0)
        return 0

    column_chunk(0, 0)
    lax.fori_loop(1, LAT, both_chunks, 0)
    merge_chunk(LAT - 1, 0)

    masks144 = head_masks(PAIR)

    def back_copy(g, half, side):
        part = pl.ds(pl.multiple_of(g * (GROUP * PAIR), GROUP * PAIR), GROUP * PAIR)
        return pltpu.make_async_remote_copy(
            src_ref=attd.at[half, part], dst_ref=back.at[half, part],
            send_sem=b_send.at[half, g], recv_sem=b_recv.at[half, g],
            device_id={"lon": side}, device_id_type=MESH,
        )

    def window_pair(p, _):
        rows = WIN * PAIR
        at = pl.multiple_of(p * rows, rows)
        quarters = []
        for band in range(2 * WIN):
            for half in range(2):
                quarters.append(wtok[pl.ds(at + half * HROWS + band * (PAIR // 2), PAIR // 2), :])
        tokens = jnp.concatenate(quarters, 0).astype(BF16)
        packed = dot(tokens, wwq_ref[...]).astype(BF16)
        bands = []
        for band in range(2 * WIN):
            one = packed[band * PAIR:(band + 1) * PAIR]
            bands.append(attend(one[:, :C], one[:, C:2 * C], one[:, 2 * C:], masks144))
        for half in range(2):
            part = slice(half * (PAIR // 2), (half + 1) * (PAIR // 2))
            attd[half, pl.ds(at, rows), :] = jnp.concatenate([b[part] for b in bands], 0).astype(BF16)
        return 0

    def window_group(g, _):
        lax.fori_loop(g * (GROUP // WIN), (g + 1) * (GROUP // WIN), window_pair, 0)
        back_copy(g, 0, east).start()
        back_copy(g, 1, west).start()
        return 0

    lax.fori_loop(0, GROUPS, window_group, 0)

    def out_copy(half, dest):
        return pltpu.make_async_remote_copy(
            src_ref=msg.at[half, dest], dst_ref=got.at[half, me],
            send_sem=o_send.at[half], recv_sem=o_recv.at[half],
            device_id={"lev": dest}, device_id_type=MESH,
        )

    for half in range(2):

        def feed_pair(p, _):
            rows = FEED * PAIR
            at = pl.multiple_of(p * rows, rows)
            attended = jnp.where(
                mask[half, pl.ds(at, rows), :] > 0,
                attd[half, pl.ds(at, rows), :].astype(F32),
                back[half, pl.ds(at, rows), :].astype(F32),
            ).astype(BF16)
            stay = after[pl.ds(at + half * HROWS, rows), :] + dot(attended, wwo_ref[...])
            hidden = gelu(dot(norm(stay, gmlp_ref[...]), wup_ref[...]))
            blk[half, pl.ds(at, rows), :] = stay + dot(hidden.astype(BF16), wdn_ref[...])
            return 0

        def feed_group(g, _):
            back_copy(g, half, east if half == 0 else west).wait_recv()
            lax.fori_loop(g * (GROUP // FEED), (g + 1) * (GROUP // FEED), feed_pair, 0)
            return 0

        blk[half, pl.ds(HROWS, PAIR), :] = jnp.zeros((PAIR, C), F32)
        lax.fori_loop(0, GROUPS, feed_group, 0)

        def block_for(dest):
            rows = blk[half, pl.ds(starts[dest] * COLS, ROWS_OUT), :]
            return jnp.where(row < counts_ref[dest] * COLS, rows, 0.0).astype(BF16)

        def send_out(step, _):
            dest = plane_target(me, LEVD - step)
            msg[half, dest] = block_for(dest)
            out_copy(half, dest).start()
            return 0

        lax.fori_loop(1, LEVD, send_out, 0)
        got[half, me] = block_for(me)

    for half in range(2):
        pltpu.make_async_copy(
            got.at[half, pl.ds(0, LEVD - 1)], got.at[half, pl.ds(0, LEVD - 1)], o_recv.at[half]
        ).wait()

        def widen_out(e, _):
            big[pl.ds(pl.multiple_of(e * ROWS_OUT, ROWS_OUT), ROWS_OUT), :] = got[half, e].astype(F32)
            return 0

        lax.fori_loop(0, LEVD, widen_out, 0)

        def unpack(n, _):
            slot, lon = n // HALF, lax.rem(n, HALF)
            for i in range(LAT):
                r32[pl.ds(i, LEVD, stride=LAT), :] = big[
                    pl.ds(slot * COLS + i * HALF + lon, LEVD, stride=ROWS_OUT), :
                ]
            out_ref[slot * LON + half * HALF + lon] = r32[pl.ds(0, LATS), :].astype(BF16)
            return 0

        lax.fori_loop(0, SLOTS * HALF, unpack, 0)

    for i in range(LAT):
        pltpu.make_async_copy(
            sendbuf.at[i, pl.ds(0, LEVD - 1)], sendbuf.at[i, pl.ds(0, LEVD - 1)], in_send.at[i]
        ).wait()
        halo_copy(i, 0, west).wait_send()
        halo_copy(i, 1, east).wait_send()
    for g in range(GROUPS):
        back_copy(g, 0, east).wait_send()
        back_copy(g, 1, west).wait_send()
    for half in range(2):
        pltpu.make_async_copy(
            msg.at[half, pl.ds(0, LEVD - 1)], msg.at[half, pl.ds(0, LEVD - 1)], o_send.at[half]
        ).wait()


def per_device(
    levels_in, slab_levels, shifts, gain_col, w_col_qkv, w_col_out, gain_win, w_win_qkv, w_win_out,
    gain_mlp, w_up, w_down,
):
    x = levels_in.transpose(0, 2, 1, 3).reshape(ROWS_IN, LATS, C)
    smem = pl.BlockSpec(memory_space=pltpu.SMEM)
    vmem = pl.BlockSpec(memory_space=pltpu.VMEM)
    dma = pltpu.SemaphoreType.DMA
    out = pl.pallas_call(
        kernel,
        out_shape=jax.ShapeDtypeStruct((ROWS_IN, LATS, C), BF16),
        in_specs=[smem, smem] + [vmem] * 10,
        out_specs=vmem,
        scratch_shapes=[
            pltpu.SMEM((LEV,), jnp.int32),
            pltpu.SMEM((LEVD,), jnp.int32),
            pltpu.VMEM((ROWS_IN * LATS, C), F32),
            pltpu.VMEM((LAT, LEVD, ROWS_IN, C), BF16),
            pltpu.VMEM((LAT, LEVD, ROWS_IN, C), BF16),
            pltpu.VMEM((LEVD * ROWS_IN + 8, C), F32),
            pltpu.VMEM((LEV * 16, C), F32),
            pltpu.VMEM((LEV, C), jnp.int32),
            pltpu.VMEM((2 * HROWS, C), F32),
            pltpu.VMEM((LAT, 2, HCOL, C), BF16),
            pltpu.VMEM((LAT, 2, HCOL, C), BF16),
            pltpu.VMEM((2 * HROWS, C), F32),
            pltpu.VMEM((2, HROWS, C), BF16),
            pltpu.VMEM((2, HROWS, C), BF16),
            pltpu.VMEM((2, HROWS, C), jnp.int32),
            pltpu.VMEM((2, HROWS + PAIR, C), F32),
            pltpu.VMEM((2, LEVD, ROWS_OUT, C), BF16),
            pltpu.VMEM((2, LEVD, ROWS_OUT, C), BF16),
            dma((LAT,)), dma((LAT,)),
            dma((LAT, 2)), dma((LAT, 2)),
            dma((2, GROUPS)), dma((2, GROUPS)),
            dma((2,)), dma((2,)),
        ],
        compiler_params=pltpu.CompilerParams(
            collective_id=0, has_side_effects=True, vmem_limit_bytes=56 * 1024 * 1024
        ),
    )(
        slab_levels, shifts, x, gain_col.reshape(1, C), w_col_qkv, w_col_out, gain_win.reshape(1, C),
        w_win_qkv, w_win_out, gain_mlp.reshape(1, C), w_up, w_down,
    )
    return out.reshape(SLOTS, LON, LATS, C).transpose(0, 2, 1, 3)


def solution(mesh):
    placed = (P("lev", None, "lon", None),) + (P(),) * 11
    return jax.shard_map(
        per_device,
        mesh=mesh,
        in_specs=placed,
        out_specs=P("lev", None, "lon", None),
        check_vma=False,
    )
```

```python
import functools
import math

import jax
import jax.numpy as jnp
from jax import lax
from jax.experimental import pallas as pl
from jax.experimental.pallas import tpu as pltpu
from jax.sharding import PartitionSpec as P

HEADS = 4
EPS = 1e-05
MESH = pl.DeviceIdType.MESH
F32 = jnp.float32
BF16 = jnp.bfloat16

SLOTS = 4
LON = 12
LAT = 6
HALF = LON // 2
LEVD = 32
LEV = 64
LATS = LAT * LEVD
C = 128
COLS = HALF * LAT
ROWS_IN = SLOTS * LON
ROWS_OUT = SLOTS * COLS
HROWS = LEV * COLS
PAIR = 4 * COLS
PAIRS = LEV // 4
GROUPS = 4
GROUP = PAIRS // GROUPS
HCOL = HALF * LEV
FEED = 4
WIN = 4
GELU_A = math.sqrt(2.0 / math.pi)
GELU_B = GELU_A * 0.044715
SCALE = math.log2(math.e) / math.sqrt(C // HEADS)


def norm(v, gain):
    centred = v - jnp.mean(v, -1, keepdims=True)
    spread = jnp.mean(centred * centred, -1, keepdims=True)
    return (centred * lax.rsqrt(spread + EPS) * gain).astype(BF16)


def dot(a, b):
    return jnp.dot(a, b, preferred_element_type=F32)


def dot_nt(a, b):
    return lax.dot_general(a, b, (((1,), (1,)), ((), ())), preferred_element_type=F32)


def head_masks(rows):
    lane = lax.broadcasted_iota(jnp.int32, (rows, C), 1)
    return [(lane // (C // HEADS)) == h for h in range(HEADS)]


def attend(q, k, v, masks):
    n = q.shape[0]
    value = jnp.concatenate([v, jnp.ones((n, C), BF16)], 1)
    over, under = None, None
    for h in range(HEADS):
        scores = dot_nt(jnp.where(masks[h], q, jnp.zeros_like(q)), k)
        top = jnp.max(scores, -1, keepdims=True)
        probs = jnp.exp2((scores - top) * SCALE).astype(BF16)
        both = dot(probs, value)
        over = both[:, :C] if h == 0 else jnp.where(masks[h], both[:, :C], over)
        under = both[:, C:] if h == 0 else jnp.where(masks[h], both[:, C:], under)
    return over / under


def attend_short(q, k, v, masks, ones):
    zero = jnp.zeros_like(k)
    keys = jnp.concatenate([jnp.where(m, k, zero) for m in masks], 0)
    values = jnp.concatenate([jnp.where(m, v, zero) for m in masks], 0)
    scores = dot_nt(q, keys)
    low = lax.broadcasted_iota(jnp.int32, (LEV, C), 1) < LEV
    probs = []
    for t in range(2):
        part = scores[:, t * C:(t + 1) * C]
        top = jnp.where(
            low,
            jnp.max(jnp.where(low, part, -jnp.inf), -1, keepdims=True),
            jnp.max(jnp.where(low, -jnp.inf, part), -1, keepdims=True),
        )
        probs.append(jnp.exp2((part - top) * SCALE).astype(BF16))
    both = dot(jnp.concatenate(probs, 1), jnp.concatenate([values, ones], 1))
    return both[:, :C] / both[:, C:]


def attend_long(q, k, v, masks, tail_masks, ones, tail_ones):
    n = q.shape[0]
    extra = n - C
    km, kt, vm, vt = k[:C], k[C:], v[:C], v[C:]
    zero, none = jnp.zeros_like(km), jnp.zeros_like(kt)
    tail = dot_nt(q, jnp.concatenate([jnp.where(m[:extra], kt, none) for m in masks], 0))
    tails = jnp.zeros((n, HEADS * extra), F32)
    total = None
    for h in range(HEADS):
        scores = dot_nt(q, jnp.where(masks[h], km, zero))
        mine = jnp.where(tail_masks[h], tail, -jnp.inf)
        top = jnp.max(jnp.maximum(scores, jnp.concatenate([mine, jnp.full((n, C - HEADS * extra), -jnp.inf, F32)], 1)), -1, keepdims=True)
        probs = jnp.exp2((scores - top) * SCALE).astype(BF16)
        tails = jnp.where(tail_masks[h], top, tails)
        part = dot(probs, jnp.concatenate([jnp.where(masks[h], vm, zero), ones[h]], 1))
        total = part if total is None else total + part
    probs = jnp.exp2((tail - tails) * SCALE).astype(BF16)
    values = jnp.concatenate([jnp.where(m[:extra], vt, none) for m in masks], 0)
    total = total + dot(probs, jnp.concatenate([values, tail_ones], 1))
    return total[:, :C] / total[:, C:]


def gelu(v):
    inner = v * (GELU_A + GELU_B * (v * v))
    half = 0.5 * v
    return half * jnp.tanh(inner) + half


def plane_target(me, step):
    core, x, y = lax.rem(me, 2), lax.rem(me // 2, 4), me // 8
    dc, dx, dy = lax.rem(step, 2), lax.rem(step // 2, 4), step // 8
    return (lax.rem(y + dy, 4) * 4 + lax.rem(x + dx, 4)) * 2 + lax.rem(core + dc, 2)


def kernel(
    counts_ref, shifts_ref, x_ref, gcol_hbm, wcq_hbm, wco_hbm, gwin_hbm, wwq_hbm, wwo_hbm,
    gmlp_hbm, wup_hbm, wdn_hbm, out_ref,
    gcol_ref, wcq_ref, wco_ref, gwin_ref, wwq_ref, wwo_ref, gmlp_ref, wup_ref, wdn_ref,
    rowoff, starts, xin, big, sendbuf, recv, r32, xl, srow, after, hsend, hrecv, wtok, attd, back,
    mask, blk, msg, got,
    x_sem, w_sem, in_send, in_recv, h_send, h_recv, b_send, b_recv, o_send, o_recv,
):
    me = lax.axis_index("lev")
    z = lax.axis_index("lon")
    east = lax.rem(z + 1, 8)
    west = lax.rem(z + 7, 8)

    barrier = pltpu.get_barrier_semaphore()

    def x_copy(slot):
        part = pl.ds(slot * LON, LON)
        return pltpu.make_async_copy(x_ref.at[part], xin.at[part], x_sem.at[slot])

    for slot in range(SLOTS):
        x_copy(slot).start()
    weights = [
        pltpu.make_async_copy(far, near, w_sem.at[n])
        for n, (far, near) in enumerate([
            (gcol_hbm, gcol_ref), (wcq_hbm, wcq_ref), (wco_hbm, wco_ref), (gwin_hbm, gwin_ref),
            (wwq_hbm, wwq_ref), (wwo_hbm, wwo_ref), (gmlp_hbm, gmlp_ref), (wup_hbm, wup_ref),
            (wdn_hbm, wdn_ref),
        ])
    ]

    def greet(step, _):
        pl.semaphore_signal(barrier, inc=1, device_id={"lev": plane_target(me, step)}, device_id_type=MESH)
        return 0

    lax.fori_loop(1, LEVD, greet, 0)
    for side in (east, west):
        pl.semaphore_signal(barrier, inc=1, device_id={"lon": side}, device_id_type=MESH)

    def widen(n, _):
        big[pl.ds(pl.multiple_of(n * LATS, LATS), LATS), :] = xin[n].astype(F32)
        return 0

    for slot in range(SLOTS):
        x_copy(slot).wait()
        lax.fori_loop(slot * LON, (slot + 1) * LON, widen, 0)
    pl.semaphore_wait(barrier, LEVD - 1 + 2)

    def in_copy(i, dest):
        return pltpu.make_async_remote_copy(
            src_ref=sendbuf.at[i, dest], dst_ref=recv.at[i, me],
            send_sem=in_send.at[i], recv_sem=in_recv.at[i],
            device_id={"lev": dest}, device_id_type=MESH,
        )

    def send_chunk(i, _):
        def one(step, _):
            dest = plane_target(me, LEVD - step)
            sendbuf[i, dest] = big[pl.ds(dest * LAT + i, ROWS_IN, stride=LATS), :].astype(BF16)
            in_copy(i, dest).start()
            return 0

        lax.fori_loop(1, LEVD, one, 0)
        recv[i, me] = big[pl.ds(me * LAT + i, ROWS_IN, stride=LATS), :].astype(BF16)
        return 0

    lax.fori_loop(0, LAT, send_chunk, 0)

    for weight in weights:
        weight.start()

    def place(level, carry):
        slab, slot = carry
        rowoff[level] = jnp.minimum(slab, LEVD - 1) * ROWS_IN + jnp.minimum(slot, SLOTS - 1) * LON
        more = slot + 1
        ends = more >= counts_ref[jnp.minimum(slab, LEVD - 1)]
        return jnp.where(ends, slab + 1, slab), jnp.where(ends, 0, more)

    lax.fori_loop(0, LEV, place, (jnp.int32(0), jnp.int32(0)))

    def begin(slab, start):
        starts[slab] = jnp.minimum(start, LEV - 1)
        return start + counts_ref[slab]

    lax.fori_loop(0, LEVD, begin, jnp.int32(0))

    def shift_rows(level, _):
        srow[pl.ds(level, 1), :] = jnp.full((1, C), shifts_ref[level // 2], jnp.int32)
        return 0

    lax.fori_loop(0, LEV, shift_rows, 0)

    row = lax.broadcasted_iota(jnp.int32, (PAIR, C), 0)

    def own_rows(p, _):
        shift = jnp.where(row < PAIR // 2, shifts_ref[2 * p], shifts_ref[2 * p + 1])
        for half in range(2):
            own = (lax.rem(row, HALF) + half * HALF >= shift) == (shift <= HALF)
            mask[half, pl.ds(pl.multiple_of(p * PAIR, PAIR), PAIR), :] = own.astype(jnp.int32)
        return 0

    lax.fori_loop(0, PAIRS, own_rows, 0)

    def halo_copy(i, half, side):
        return pltpu.make_async_remote_copy(
            src_ref=hsend.at[i, half], dst_ref=hrecv.at[i, half],
            send_sem=h_send.at[i, half], recv_sem=h_recv.at[i, half],
            device_id={"lon": side}, device_id_type=MESH,
        )

    masks64 = head_masks(LEV)
    ones64 = jnp.concatenate([m.astype(BF16) for m in masks64], 0)

    def column_chunk(i, _):
        pltpu.make_async_copy(
            recv.at[i, pl.ds(0, LEVD - 1)], recv.at[i, pl.ds(0, LEVD - 1)], in_recv.at[i]
        ).wait()

        def widen_in(d, _):
            r32[pl.ds(pl.multiple_of(d * ROWS_IN, ROWS_IN), ROWS_IN), :] = recv[i, d].astype(F32)
            return 0

        lax.fori_loop(0, LEVD, widen_in, 0, unroll=4)

        def pick(level, _):
            xl[pl.ds(pl.multiple_of(level * 16, 16), 16), :] = r32[pl.ds(rowoff[level], 16), :]
            return 0

        lax.fori_loop(0, LEV, pick, 0, unroll=16)

        cols = jnp.concatenate([xl[pl.ds(lon, LEV, stride=16), :] for lon in range(LON)], 0)
        packed = dot(norm(cols, gcol_ref[...]), wcq_ref[...]).astype(BF16)
        parts = []
        for n in range(LON):
            one = packed[n * LEV:(n + 1) * LEV]
            parts.append(attend_short(one[:, :C], one[:, C:2 * C], one[:, 2 * C:], masks64, ones64))
        done = cols + dot(jnp.concatenate(parts, 0).astype(BF16), wco_ref[...])
        normed = norm(done, gwin_ref[...])
        for half in range(2):
            for n in range(HALF):
                part = slice((half * HALF + n) * LEV, (half * HALF + n + 1) * LEV)
                after[pl.ds(half * HROWS + i * HALF + n, LEV, stride=COLS), :] = done[part]
                hsend[i, half, pl.ds(n * LEV, LEV), :] = normed[part]
            halo_copy(i, half, west if half == 0 else east).start()
        return 0

    def merge_chunk(i, _):
        for half in range(2):
            halo_copy(i, half, west if half == 0 else east).wait_recv()
            for n in range(HALF):
                lon = half * HALF + n
                shift = srow[...]
                own = (lon >= shift) == (shift <= HALF)
                mine = hsend[i, half, pl.ds(n * LEV, LEV), :].astype(F32)
                other = hrecv[i, half, pl.ds(n * LEV, LEV), :].astype(F32)
                at = half * HROWS + i * HALF + n
                wtok[pl.ds(at, LEV, stride=COLS), :] = jnp.where(own, mine, other)
        return 0

    def both_chunks(i, _):
        column_chunk(i, 0)
        merge_chunk(i - 1, 0)
        return 0

    for weight in weights:
        weight.wait()
    column_chunk(0, 0)
    lax.fori_loop(1, LAT, both_chunks, 0)
    merge_chunk(LAT - 1, 0)

    masks144 = head_masks(PAIR)

    def back_copy(g, half, side):
        part = pl.ds(pl.multiple_of(g * (GROUP * PAIR), GROUP * PAIR), GROUP * PAIR)
        return pltpu.make_async_remote_copy(
            src_ref=attd.at[half, part], dst_ref=back.at[half, part],
            send_sem=b_send.at[half, g], recv_sem=b_recv.at[half, g],
            device_id={"lon": side}, device_id_type=MESH,
        )

    def window_pair(p, _):
        rows = WIN * PAIR
        at = pl.multiple_of(p * rows, rows)
        quarters = []
        for band in range(2 * WIN):
            for half in range(2):
                quarters.append(wtok[pl.ds(at + half * HROWS + band * (PAIR // 2), PAIR // 2), :])
        tokens = jnp.concatenate(quarters, 0).astype(BF16)
        packed = dot(tokens, wwq_ref[...]).astype(BF16)
        bands = []
        for band in range(2 * WIN):
            one = packed[band * PAIR:(band + 1) * PAIR]
            bands.append(attend(one[:, :C], one[:, C:2 * C], one[:, 2 * C:], masks144))
        for half in range(2):
            part = slice(half * (PAIR // 2), (half + 1) * (PAIR // 2))
            attd[half, pl.ds(at, rows), :] = jnp.concatenate([b[part] for b in bands], 0).astype(BF16)
        return 0

    def window_group(g, _):
        lax.fori_loop(g * (GROUP // WIN), (g + 1) * (GROUP // WIN), window_pair, 0)
        back_copy(g, 0, east).start()
        back_copy(g, 1, west).start()
        return 0

    lax.fori_loop(0, GROUPS, window_group, 0)

    def out_copy(half, dest):
        return pltpu.make_async_remote_copy(
            src_ref=msg.at[half, dest], dst_ref=got.at[half, me],
            send_sem=o_send.at[half], recv_sem=o_recv.at[half],
            device_id={"lev": dest}, device_id_type=MESH,
        )

    for half in range(2):

        def feed_pair(p, _):
            rows = FEED * PAIR
            at = pl.multiple_of(p * rows, rows)
            attended = jnp.where(
                mask[half, pl.ds(at, rows), :] > 0,
                attd[half, pl.ds(at, rows), :].astype(F32),
                back[half, pl.ds(at, rows), :].astype(F32),
            ).astype(BF16)
            stay = after[pl.ds(at + half * HROWS, rows), :] + dot(attended, wwo_ref[...])
            hidden = gelu(dot(norm(stay, gmlp_ref[...]), wup_ref[...]))
            blk[half, pl.ds(at, rows), :] = stay + dot(hidden.astype(BF16), wdn_ref[...])
            return 0

        def feed_group(g, _):
            back_copy(g, half, east if half == 0 else west).wait_recv()
            lax.fori_loop(g * (GROUP // FEED), (g + 1) * (GROUP // FEED), feed_pair, 0)
            return 0

        blk[half, pl.ds(HROWS, PAIR), :] = jnp.zeros((PAIR, C), F32)
        lax.fori_loop(0, GROUPS, feed_group, 0)

        def block_for(dest):
            rows = blk[half, pl.ds(starts[dest] * COLS, ROWS_OUT), :]
            return jnp.where(row < counts_ref[dest] * COLS, rows, 0.0).astype(BF16)

        def send_out(step, _):
            dest = plane_target(me, LEVD - step)
            msg[half, dest] = block_for(dest)
            out_copy(half, dest).start()
            return 0

        lax.fori_loop(1, LEVD, send_out, 0)
        got[half, me] = block_for(me)

    for half in range(2):
        pltpu.make_async_copy(
            got.at[half, pl.ds(0, LEVD - 1)], got.at[half, pl.ds(0, LEVD - 1)], o_recv.at[half]
        ).wait()

        def widen_out(e, _):
            big[pl.ds(pl.multiple_of(e * ROWS_OUT, ROWS_OUT), ROWS_OUT), :] = got[half, e].astype(F32)
            return 0

        lax.fori_loop(0, LEVD, widen_out, 0)

        def unpack(n, _):
            slot, lon = n // HALF, lax.rem(n, HALF)
            for i in range(LAT):
                r32[pl.ds(i, LEVD, stride=LAT), :] = big[
                    pl.ds(slot * COLS + i * HALF + lon, LEVD, stride=ROWS_OUT), :
                ]
            at = slot * LON + half * HALF + lon
            out_ref[at] = r32[pl.ds(0, LATS), :].astype(BF16)
            return 0

        lax.fori_loop(0, SLOTS * HALF, unpack, 0)

    for i in range(LAT):
        pltpu.make_async_copy(
            sendbuf.at[i, pl.ds(0, LEVD - 1)], sendbuf.at[i, pl.ds(0, LEVD - 1)], in_send.at[i]
        ).wait()
        halo_copy(i, 0, west).wait_send()
        halo_copy(i, 1, east).wait_send()
    for g in range(GROUPS):
        back_copy(g, 0, east).wait_send()
        back_copy(g, 1, west).wait_send()
    for half in range(2):
        pltpu.make_async_copy(
            msg.at[half, pl.ds(0, LEVD - 1)], msg.at[half, pl.ds(0, LEVD - 1)], o_send.at[half]
        ).wait()


def per_device(
    levels_in, slab_levels, shifts, gain_col, w_col_qkv, w_col_out, gain_win, w_win_qkv, w_win_out,
    gain_mlp, w_up, w_down,
):
    x = levels_in.transpose(0, 2, 1, 3).reshape(ROWS_IN, LATS, C)
    weights = [
        gain_col.reshape(1, C), w_col_qkv, w_col_out, gain_win.reshape(1, C), w_win_qkv, w_win_out,
        gain_mlp.reshape(1, C), w_up, w_down,
    ]
    smem = pl.BlockSpec(memory_space=pltpu.SMEM)
    vmem = pl.BlockSpec(memory_space=pltpu.VMEM)
    dma = pltpu.SemaphoreType.DMA
    out = pl.pallas_call(
        kernel,
        out_shape=pltpu.VMEM((ROWS_IN, LATS, C), BF16),
        in_specs=[smem, smem] + [pl.BlockSpec(memory_space=pl.ANY)] * 10,
        out_specs=vmem,
        scratch_shapes=[
            *[pltpu.VMEM(w.shape, w.dtype) for w in weights],
            pltpu.SMEM((LEV,), jnp.int32),
            pltpu.SMEM((LEVD,), jnp.int32),
            pltpu.VMEM((ROWS_IN, LATS, C), BF16),
            pltpu.VMEM((ROWS_IN * LATS, C), F32),
            pltpu.VMEM((LAT, LEVD, ROWS_IN, C), BF16),
            pltpu.VMEM((LAT, LEVD, ROWS_IN, C), BF16),
            pltpu.VMEM((LEVD * ROWS_IN + 8, C), F32),
            pltpu.VMEM((LEV * 16, C), F32),
            pltpu.VMEM((LEV, C), jnp.int32),
            pltpu.VMEM((2 * HROWS, C), F32),
            pltpu.VMEM((LAT, 2, HCOL, C), BF16),
            pltpu.VMEM((LAT, 2, HCOL, C), BF16),
            pltpu.VMEM((2 * HROWS, C), F32),
            pltpu.VMEM((2, HROWS, C), BF16),
            pltpu.VMEM((2, HROWS, C), BF16),
            pltpu.VMEM((2, HROWS, C), jnp.int32),
            pltpu.VMEM((2, HROWS + PAIR, C), F32),
            pltpu.VMEM((2, LEVD, ROWS_OUT, C), BF16),
            pltpu.VMEM((2, LEVD, ROWS_OUT, C), BF16),
            dma((SLOTS,)), dma((9,)),
            dma((LAT,)), dma((LAT,)),
            dma((LAT, 2)), dma((LAT, 2)),
            dma((2, GROUPS)), dma((2, GROUPS)),
            dma((2,)), dma((2,)),
        ],
        compiler_params=pltpu.CompilerParams(
            collective_id=0, has_side_effects=True, vmem_limit_bytes=56 * 1024 * 1024
        ),
    )(slab_levels, shifts, x, *weights)
    return out.reshape(SLOTS, LON, LATS, C).transpose(0, 2, 1, 3)


def solution(mesh):
    placed = (P("lev", None, "lon", None),) + (P(),) * 11
    return jax.shard_map(
        per_device,
        mesh=mesh,
        in_specs=placed,
        out_specs=P("lev", None, "lon", None),
        check_vma=False,
    )
```

```python
import functools
import math

import jax
import jax.numpy as jnp
from jax import lax
from jax.experimental import pallas as pl
from jax.experimental.pallas import tpu as pltpu
from jax.sharding import PartitionSpec as P

HEADS = 4
EPS = 1e-05
MESH = pl.DeviceIdType.MESH
F32 = jnp.float32
BF16 = jnp.bfloat16

SLOTS = 4
LON = 12
LAT = 6
HALF = LON // 2
LEVD = 32
LEV = 64
LATS = LAT * LEVD
C = 128
COLS = HALF * LAT
ROWS_IN = SLOTS * LON
ROWS_OUT = SLOTS * COLS
HROWS = LEV * COLS
PAIR = 4 * COLS
PAIRS = LEV // 4
GROUPS = 4
GROUP = PAIRS // GROUPS
HCOL = HALF * LEV
FEED = 4
WIN = 4
GELU_A = math.sqrt(2.0 / math.pi)
GELU_B = GELU_A * 0.044715
SCALE = math.log2(math.e) / math.sqrt(C // HEADS)


def norm(v, gain):
    centred = v - jnp.mean(v, -1, keepdims=True)
    spread = jnp.mean(centred * centred, -1, keepdims=True)
    return (centred * lax.rsqrt(spread + EPS) * gain).astype(BF16)


def dot(a, b):
    return jnp.dot(a, b, preferred_element_type=F32)


def dot_nt(a, b):
    return lax.dot_general(a, b, (((1,), (1,)), ((), ())), preferred_element_type=F32)


def head_masks(rows):
    lane = lax.broadcasted_iota(jnp.int32, (rows, C), 1)
    return [(lane // (C // HEADS)) == h for h in range(HEADS)]


def attend(q, k, v, masks):
    n = q.shape[0]
    value = jnp.concatenate([v, jnp.ones((n, C), BF16)], 1)
    over, under = None, None
    for h in range(HEADS):
        scores = dot_nt(jnp.where(masks[h], q, jnp.zeros_like(q)), k)
        top = jnp.max(scores, -1, keepdims=True)
        probs = jnp.exp2((scores - top) * SCALE).astype(BF16)
        both = dot(probs, value)
        over = both[:, :C] if h == 0 else jnp.where(masks[h], both[:, :C], over)
        under = both[:, C:] if h == 0 else jnp.where(masks[h], both[:, C:], under)
    return over / under


def attend_short(q, k, v, masks, ones):
    zero = jnp.zeros_like(k)
    keys = jnp.concatenate([jnp.where(m, k, zero) for m in masks], 0)
    values = jnp.concatenate([jnp.where(m, v, zero) for m in masks], 0)
    scores = dot_nt(q, keys)
    low = lax.broadcasted_iota(jnp.int32, (LEV, C), 1) < LEV
    probs = []
    for t in range(2):
        part = scores[:, t * C:(t + 1) * C]
        top = jnp.where(
            low,
            jnp.max(jnp.where(low, part, -jnp.inf), -1, keepdims=True),
            jnp.max(jnp.where(low, -jnp.inf, part), -1, keepdims=True),
        )
        probs.append(jnp.exp2((part - top) * SCALE).astype(BF16))
    both = dot(jnp.concatenate(probs, 1), jnp.concatenate([values, ones], 1))
    return both[:, :C] / both[:, C:]


def attend_long(q, k, v, masks, tail_masks, ones, tail_ones):
    n = q.shape[0]
    extra = n - C
    km, kt, vm, vt = k[:C], k[C:], v[:C], v[C:]
    zero, none = jnp.zeros_like(km), jnp.zeros_like(kt)
    tail = dot_nt(q, jnp.concatenate([jnp.where(m[:extra], kt, none) for m in masks], 0))
    tails = jnp.zeros((n, HEADS * extra), F32)
    total = None
    for h in range(HEADS):
        scores = dot_nt(q, jnp.where(masks[h], km, zero))
        mine = jnp.where(tail_masks[h], tail, -jnp.inf)
        top = jnp.max(jnp.maximum(scores, jnp.concatenate([mine, jnp.full((n, C - HEADS * extra), -jnp.inf, F32)], 1)), -1, keepdims=True)
        probs = jnp.exp2((scores - top) * SCALE).astype(BF16)
        tails = jnp.where(tail_masks[h], top, tails)
        part = dot(probs, jnp.concatenate([jnp.where(masks[h], vm, zero), ones[h]], 1))
        total = part if total is None else total + part
    probs = jnp.exp2((tail - tails) * SCALE).astype(BF16)
    values = jnp.concatenate([jnp.where(m[:extra], vt, none) for m in masks], 0)
    total = total + dot(probs, jnp.concatenate([values, tail_ones], 1))
    return total[:, :C] / total[:, C:]


def gelu(v):
    inner = v * (GELU_A + GELU_B * (v * v))
    half = 0.5 * v
    return half * jnp.tanh(inner) + half


CHIPS = (
    (2, 2), (2, 1), (1, 2), (2, 3), (3, 2), (1, 1), (3, 3), (1, 3), (3, 1), (2, 0), (0, 2),
    (0, 1), (0, 3), (1, 0), (3, 0), (0, 0),
)


def chip_at(me, dy, dx):
    x, y = lax.rem(me // 2, 4), me // 8
    return (lax.rem(y + dy, 4) * 4 + lax.rem(x + dx, 4)) * 2


def kernel(
    counts_ref, shifts_ref, x_ref, gcol_hbm, wcq_hbm, wco_hbm, gwin_hbm, wwq_hbm, wwo_hbm,
    gmlp_hbm, wup_hbm, wdn_hbm, out_ref,
    gcol_ref, wcq_ref, wco_ref, gwin_ref, wwq_ref, wwo_ref, gmlp_ref, wup_ref, wdn_ref,
    rowoff, starts, xin, big, sendbuf, recv, r32, xl, srow, after, hsend, hrecv, wtok, attd, back,
    mask, blk, msg, got,
    x_sem, w_sem, in_send, in_recv, h_send, h_recv, b_send, b_recv, o_send, o_recv,
):
    me = lax.axis_index("lev")
    z = lax.axis_index("lon")
    east = lax.rem(z + 1, 8)
    west = lax.rem(z + 7, 8)

    barrier = pltpu.get_barrier_semaphore()

    def x_copy(slot):
        part = pl.ds(slot * LON, LON)
        return pltpu.make_async_copy(x_ref.at[part], xin.at[part], x_sem.at[slot])

    for slot in range(SLOTS):
        x_copy(slot).start()
    weights = [
        pltpu.make_async_copy(far, near, w_sem.at[n])
        for n, (far, near) in enumerate([
            (gcol_hbm, gcol_ref), (wcq_hbm, wcq_ref), (wco_hbm, wco_ref), (gwin_hbm, gwin_ref),
            (wwq_hbm, wwq_ref), (wwo_hbm, wwo_ref), (gmlp_hbm, gmlp_ref), (wup_hbm, wup_ref),
            (wdn_hbm, wdn_ref),
        ])
    ]

    def greet(step, _):
        pl.semaphore_signal(barrier, inc=1, device_id={"lev": lax.rem(me + step, LEVD)}, device_id_type=MESH)
        return 0

    lax.fori_loop(1, LEVD, greet, 0)
    for side in (east, west):
        pl.semaphore_signal(barrier, inc=1, device_id={"lon": side}, device_id_type=MESH)

    def widen(n, _):
        big[pl.ds(pl.multiple_of(n * LATS, LATS), LATS), :] = xin[n].astype(F32)
        return 0

    for slot in range(SLOTS):
        x_copy(slot).wait()
        lax.fori_loop(slot * LON, (slot + 1) * LON, widen, 0)
    pl.semaphore_wait(barrier, LEVD - 1 + 2)

    def in_copy(i, dest):
        return pltpu.make_async_remote_copy(
            src_ref=sendbuf.at[i, dest], dst_ref=recv.at[i, me],
            send_sem=in_send.at[i], recv_sem=in_recv.at[i],
            device_id={"lev": dest}, device_id_type=MESH,
        )

    core = lax.rem(me, 2)
    mate = me + 1 - 2 * core

    def send_to(i, dest):
        sendbuf[i, dest] = big[pl.ds(dest * LAT + i, ROWS_IN, stride=LATS), :].astype(BF16)
        in_copy(i, dest).start()

    def send_chunk(i, _, turn):
        for dy, dx in CHIPS[:-1]:
            send_to(i, chip_at(me, dy, dx) + turn)

        @pl.when(core != turn)
        def _():
            send_to(i, mate)

        return 0

    def keep_chunk(i, _):
        recv[i, me] = big[pl.ds(me * LAT + i, ROWS_IN, stride=LATS), :].astype(BF16)
        return 0

    lax.fori_loop(0, LAT, functools.partial(send_chunk, turn=0), 0)

    lax.fori_loop(0, LAT, functools.partial(send_chunk, turn=1), 0)

    lax.fori_loop(0, LAT, keep_chunk, 0)

    for weight in weights:
        weight.start()

    def place(level, carry):
        slab, slot = carry
        rowoff[level] = jnp.minimum(slab, LEVD - 1) * ROWS_IN + jnp.minimum(slot, SLOTS - 1) * LON
        more = slot + 1
        ends = more >= counts_ref[jnp.minimum(slab, LEVD - 1)]
        return jnp.where(ends, slab + 1, slab), jnp.where(ends, 0, more)

    lax.fori_loop(0, LEV, place, (jnp.int32(0), jnp.int32(0)))

    def begin(slab, start):
        starts[slab] = jnp.minimum(start, LEV - 1)
        return start + counts_ref[slab]

    lax.fori_loop(0, LEVD, begin, jnp.int32(0))

    def shift_rows(level, _):
        srow[pl.ds(level, 1), :] = jnp.full((1, C), shifts_ref[level // 2], jnp.int32)
        return 0

    lax.fori_loop(0, LEV, shift_rows, 0)

    row = lax.broadcasted_iota(jnp.int32, (PAIR, C), 0)

    def own_rows(p, _):
        shift = jnp.where(row < PAIR // 2, shifts_ref[2 * p], shifts_ref[2 * p + 1])
        for half in range(2):
            own = (lax.rem(row, HALF) + half * HALF >= shift) == (shift <= HALF)
            mask[half, pl.ds(pl.multiple_of(p * PAIR, PAIR), PAIR), :] = own.astype(jnp.int32)
        return 0

    lax.fori_loop(0, PAIRS, own_rows, 0)

    def halo_copy(i, half, side):
        return pltpu.make_async_remote_copy(
            src_ref=hsend.at[i, half], dst_ref=hrecv.at[i, half],
            send_sem=h_send.at[i, half], recv_sem=h_recv.at[i, half],
            device_id={"lon": side}, device_id_type=MESH,
        )

    masks64 = head_masks(LEV)
    ones64 = jnp.concatenate([m.astype(BF16) for m in masks64], 0)

    def column_chunk(i, _):
        pltpu.make_async_copy(
            recv.at[i, pl.ds(0, LEVD - 1)], recv.at[i, pl.ds(0, LEVD - 1)], in_recv.at[i]
        ).wait()

        def widen_in(d, _):
            r32[pl.ds(pl.multiple_of(d * ROWS_IN, ROWS_IN), ROWS_IN), :] = recv[i, d].astype(F32)
            return 0

        lax.fori_loop(0, LEVD, widen_in, 0, unroll=4)

        def pick(level, _):
            xl[pl.ds(pl.multiple_of(level * 16, 16), 16), :] = r32[pl.ds(rowoff[level], 16), :]
            return 0

        lax.fori_loop(0, LEV, pick, 0, unroll=16)

        cols = jnp.concatenate([xl[pl.ds(lon, LEV, stride=16), :] for lon in range(LON)], 0)
        packed = dot(norm(cols, gcol_ref[...]), wcq_ref[...]).astype(BF16)
        parts = []
        for n in range(LON):
            one = packed[n * LEV:(n + 1) * LEV]
            parts.append(attend_short(one[:, :C], one[:, C:2 * C], one[:, 2 * C:], masks64, ones64))
        done = cols + dot(jnp.concatenate(parts, 0).astype(BF16), wco_ref[...])
        normed = norm(done, gwin_ref[...])
        for half in range(2):
            for n in range(HALF):
                part = slice((half * HALF + n) * LEV, (half * HALF + n + 1) * LEV)
                after[pl.ds(half * HROWS + i * HALF + n, LEV, stride=COLS), :] = done[part]
                hsend[i, half, pl.ds(n * LEV, LEV), :] = normed[part]
            halo_copy(i, half, west if half == 0 else east).start()
        return 0

    def merge_chunk(i, _):
        for half in range(2):
            halo_copy(i, half, west if half == 0 else east).wait_recv()
            for n in range(HALF):
                lon = half * HALF + n
                shift = srow[...]
                own = (lon >= shift) == (shift <= HALF)
                mine = hsend[i, half, pl.ds(n * LEV, LEV), :].astype(F32)
                other = hrecv[i, half, pl.ds(n * LEV, LEV), :].astype(F32)
                at = half * HROWS + i * HALF + n
                wtok[pl.ds(at, LEV, stride=COLS), :] = jnp.where(own, mine, other)
        return 0

    def both_chunks(i, _):
        column_chunk(i, 0)
        merge_chunk(i - 1, 0)
        return 0

    for weight in weights:
        weight.wait()
    column_chunk(0, 0)
    lax.fori_loop(1, LAT, both_chunks, 0)
    merge_chunk(LAT - 1, 0)

    masks144 = head_masks(PAIR)

    def back_copy(g, half, side):
        part = pl.ds(pl.multiple_of(g * (GROUP * PAIR), GROUP * PAIR), GROUP * PAIR)
        return pltpu.make_async_remote_copy(
            src_ref=attd.at[half, part], dst_ref=back.at[half, part],
            send_sem=b_send.at[half, g], recv_sem=b_recv.at[half, g],
            device_id={"lon": side}, device_id_type=MESH,
        )

    def window_pair(p, _):
        rows = WIN * PAIR
        at = pl.multiple_of(p * rows, rows)
        quarters = []
        for band in range(2 * WIN):
            for half in range(2):
                quarters.append(wtok[pl.ds(at + half * HROWS + band * (PAIR // 2), PAIR // 2), :])
        tokens = jnp.concatenate(quarters, 0).astype(BF16)
        packed = dot(tokens, wwq_ref[...]).astype(BF16)
        bands = []
        for band in range(2 * WIN):
            one = packed[band * PAIR:(band + 1) * PAIR]
            bands.append(attend(one[:, :C], one[:, C:2 * C], one[:, 2 * C:], masks144))
        for half in range(2):
            part = slice(half * (PAIR // 2), (half + 1) * (PAIR // 2))
            attd[half, pl.ds(at, rows), :] = jnp.concatenate([b[part] for b in bands], 0).astype(BF16)
        return 0

    def window_group(g, _):
        lax.fori_loop(g * (GROUP // WIN), (g + 1) * (GROUP // WIN), window_pair, 0)
        back_copy(g, 0, east).start()
        back_copy(g, 1, west).start()
        return 0

    lax.fori_loop(0, GROUPS, window_group, 0)

    def out_copy(half, dest):
        return pltpu.make_async_remote_copy(
            src_ref=msg.at[half, dest], dst_ref=got.at[half, me],
            send_sem=o_send.at[half], recv_sem=o_recv.at[half],
            device_id={"lev": dest}, device_id_type=MESH,
        )

    for half in range(2):

        def feed_pair(p, _):
            rows = FEED * PAIR
            at = pl.multiple_of(p * rows, rows)
            attended = jnp.where(
                mask[half, pl.ds(at, rows), :] > 0,
                attd[half, pl.ds(at, rows), :].astype(F32),
                back[half, pl.ds(at, rows), :].astype(F32),
            ).astype(BF16)
            stay = after[pl.ds(at + half * HROWS, rows), :] + dot(attended, wwo_ref[...])
            hidden = gelu(dot(norm(stay, gmlp_ref[...]), wup_ref[...]))
            blk[half, pl.ds(at, rows), :] = stay + dot(hidden.astype(BF16), wdn_ref[...])
            return 0

        def feed_group(g, _):
            back_copy(g, half, east if half == 0 else west).wait_recv()
            lax.fori_loop(g * (GROUP // FEED), (g + 1) * (GROUP // FEED), feed_pair, 0)
            return 0

        blk[half, pl.ds(HROWS, PAIR), :] = jnp.zeros((PAIR, C), F32)
        lax.fori_loop(0, GROUPS, feed_group, 0)

        def block_for(dest):
            rows = blk[half, pl.ds(starts[dest] * COLS, ROWS_OUT), :]
            return jnp.where(row < counts_ref[dest] * COLS, rows, 0.0).astype(BF16)

        def fill(dest, _):
            msg[half, dest] = block_for(dest)
            return 0

        lax.fori_loop(0, LEVD, fill, 0)
        for dy, dx in CHIPS[:-1]:
            for turn in range(2):
                out_copy(half, chip_at(me, dy, dx) + turn).start()
        out_copy(half, mate).start()
        got[half, me] = msg[half, me]

    for half in range(2):
        pltpu.make_async_copy(
            got.at[half, pl.ds(0, LEVD - 1)], got.at[half, pl.ds(0, LEVD - 1)], o_recv.at[half]
        ).wait()

        def widen_out(e, _):
            big[pl.ds(pl.multiple_of(e * ROWS_OUT, ROWS_OUT), ROWS_OUT), :] = got[half, e].astype(F32)
            return 0

        lax.fori_loop(0, LEVD, widen_out, 0)

        def unpack(n, _):
            slot, lon = n // HALF, lax.rem(n, HALF)
            for i in range(LAT):
                r32[pl.ds(i, LEVD, stride=LAT), :] = big[
                    pl.ds(slot * COLS + i * HALF + lon, LEVD, stride=ROWS_OUT), :
                ]
            at = slot * LON + half * HALF + lon
            out_ref[at] = r32[pl.ds(0, LATS), :].astype(BF16)
            return 0

        lax.fori_loop(0, SLOTS * HALF, unpack, 0)

    for i in range(LAT):
        pltpu.make_async_copy(
            sendbuf.at[i, pl.ds(0, LEVD - 1)], sendbuf.at[i, pl.ds(0, LEVD - 1)], in_send.at[i]
        ).wait()
        halo_copy(i, 0, west).wait_send()
        halo_copy(i, 1, east).wait_send()
    for g in range(GROUPS):
        back_copy(g, 0, east).wait_send()
        back_copy(g, 1, west).wait_send()
    for half in range(2):
        pltpu.make_async_copy(
            msg.at[half, pl.ds(0, LEVD - 1)], msg.at[half, pl.ds(0, LEVD - 1)], o_send.at[half]
        ).wait()


def per_device(
    levels_in, slab_levels, shifts, gain_col, w_col_qkv, w_col_out, gain_win, w_win_qkv, w_win_out,
    gain_mlp, w_up, w_down,
):
    x = levels_in.transpose(0, 2, 1, 3).reshape(ROWS_IN, LATS, C)
    weights = [
        gain_col.reshape(1, C), w_col_qkv, w_col_out, gain_win.reshape(1, C), w_win_qkv, w_win_out,
        gain_mlp.reshape(1, C), w_up, w_down,
    ]
    smem = pl.BlockSpec(memory_space=pltpu.SMEM)
    vmem = pl.BlockSpec(memory_space=pltpu.VMEM)
    dma = pltpu.SemaphoreType.DMA
    out = pl.pallas_call(
        kernel,
        out_shape=pltpu.VMEM((ROWS_IN, LATS, C), BF16),
        in_specs=[smem, smem] + [pl.BlockSpec(memory_space=pl.ANY)] * 10,
        out_specs=vmem,
        scratch_shapes=[
            *[pltpu.VMEM(w.shape, w.dtype) for w in weights],
            pltpu.SMEM((LEV,), jnp.int32),
            pltpu.SMEM((LEVD,), jnp.int32),
            pltpu.VMEM((ROWS_IN, LATS, C), BF16),
            pltpu.VMEM((ROWS_IN * LATS, C), F32),
            pltpu.VMEM((LAT, LEVD, ROWS_IN, C), BF16),
            pltpu.VMEM((LAT, LEVD, ROWS_IN, C), BF16),
            pltpu.VMEM((LEVD * ROWS_IN + 8, C), F32),
            pltpu.VMEM((LEV * 16, C), F32),
            pltpu.VMEM((LEV, C), jnp.int32),
            pltpu.VMEM((2 * HROWS, C), F32),
            pltpu.VMEM((LAT, 2, HCOL, C), BF16),
            pltpu.VMEM((LAT, 2, HCOL, C), BF16),
            pltpu.VMEM((2 * HROWS, C), F32),
            pltpu.VMEM((2, HROWS, C), BF16),
            pltpu.VMEM((2, HROWS, C), BF16),
            pltpu.VMEM((2, HROWS, C), jnp.int32),
            pltpu.VMEM((2, HROWS + PAIR, C), F32),
            pltpu.VMEM((2, LEVD, ROWS_OUT, C), BF16),
            pltpu.VMEM((2, LEVD, ROWS_OUT, C), BF16),
            dma((SLOTS,)), dma((9,)),
            dma((LAT,)), dma((LAT,)),
            dma((LAT, 2)), dma((LAT, 2)),
            dma((2, GROUPS)), dma((2, GROUPS)),
            dma((2,)), dma((2,)),
        ],
        compiler_params=pltpu.CompilerParams(
            collective_id=0, has_side_effects=True, vmem_limit_bytes=56 * 1024 * 1024
        ),
    )(slab_levels, shifts, x, *weights)
    return out.reshape(SLOTS, LON, LATS, C).transpose(0, 2, 1, 3)


def solution(mesh):
    placed = (P("lev", None, "lon", None),) + (P(),) * 11
    return jax.shard_map(
        per_device,
        mesh=mesh,
        in_specs=placed,
        out_specs=P("lev", None, "lon", None),
        check_vma=False,
    )
```

```python
import functools
import math

import jax
import jax.numpy as jnp
from jax import lax
from jax.experimental import pallas as pl
from jax.experimental.pallas import tpu as pltpu
from jax.sharding import PartitionSpec as P

HEADS = 4
EPS = 1e-05
MESH = pl.DeviceIdType.MESH
F32 = jnp.float32
BF16 = jnp.bfloat16

SLOTS = 4
LON = 12
LAT = 6
HALF = LON // 2
LEVD = 32
LEV = 64
LATS = LAT * LEVD
C = 128
COLS = HALF * LAT
ROWS_IN = SLOTS * LON
ROWS_OUT = SLOTS * COLS
HROWS = LEV * COLS
PAIR = 4 * COLS
PAIRS = LEV // 4
GROUPS = 4
GROUP = PAIRS // GROUPS
HCOL = HALF * LEV
FEED = 4
WIN = 4
GELU_A = math.sqrt(2.0 / math.pi)
GELU_B = GELU_A * 0.044715
SCALE = math.log2(math.e) / math.sqrt(C // HEADS)


def norm(v, gain):
    centred = v - jnp.mean(v, -1, keepdims=True)
    spread = jnp.mean(centred * centred, -1, keepdims=True)
    return (centred * lax.rsqrt(spread + EPS) * gain).astype(BF16)


def dot(a, b):
    return jnp.dot(a, b, preferred_element_type=F32)


def dot_nt(a, b):
    return lax.dot_general(a, b, (((1,), (1,)), ((), ())), preferred_element_type=F32)


def head_masks(rows):
    lane = lax.broadcasted_iota(jnp.int32, (rows, C), 1)
    return [(lane // (C // HEADS)) == h for h in range(HEADS)]


def attend(q, k, v, masks):
    n = q.shape[0]
    value = jnp.concatenate([v, jnp.ones((n, C), BF16)], 1)
    over, under = None, None
    for h in range(HEADS):
        scores = dot_nt(jnp.where(masks[h], q, jnp.zeros_like(q)), k)
        top = jnp.max(scores, -1, keepdims=True)
        probs = jnp.exp2((scores - top) * SCALE).astype(BF16)
        both = dot(probs, value)
        over = both[:, :C] if h == 0 else jnp.where(masks[h], both[:, :C], over)
        under = both[:, C:] if h == 0 else jnp.where(masks[h], both[:, C:], under)
    return over / under


def attend_short(q, k, v, masks, ones):
    zero = jnp.zeros_like(k)
    keys = jnp.concatenate([jnp.where(m, k, zero) for m in masks], 0)
    values = jnp.concatenate([jnp.where(m, v, zero) for m in masks], 0)
    scores = dot_nt(q, keys)
    low = lax.broadcasted_iota(jnp.int32, (LEV, C), 1) < LEV
    probs = []
    for t in range(2):
        part = scores[:, t * C:(t + 1) * C]
        top = jnp.where(
            low,
            jnp.max(jnp.where(low, part, -jnp.inf), -1, keepdims=True),
            jnp.max(jnp.where(low, -jnp.inf, part), -1, keepdims=True),
        )
        probs.append(jnp.exp2((part - top) * SCALE).astype(BF16))
    both = dot(jnp.concatenate(probs, 1), jnp.concatenate([values, ones], 1))
    return both[:, :C] / both[:, C:]


def attend_long(q, k, v, masks, tail_masks, ones, tail_ones):
    n = q.shape[0]
    extra = n - C
    km, kt, vm, vt = k[:C], k[C:], v[:C], v[C:]
    zero, none = jnp.zeros_like(km), jnp.zeros_like(kt)
    tail = dot_nt(q, jnp.concatenate([jnp.where(m[:extra], kt, none) for m in masks], 0))
    tails = jnp.zeros((n, HEADS * extra), F32)
    total = None
    for h in range(HEADS):
        scores = dot_nt(q, jnp.where(masks[h], km, zero))
        mine = jnp.where(tail_masks[h], tail, -jnp.inf)
        top = jnp.max(jnp.maximum(scores, jnp.concatenate([mine, jnp.full((n, C - HEADS * extra), -jnp.inf, F32)], 1)), -1, keepdims=True)
        probs = jnp.exp2((scores - top) * SCALE).astype(BF16)
        tails = jnp.where(tail_masks[h], top, tails)
        part = dot(probs, jnp.concatenate([jnp.where(masks[h], vm, zero), ones[h]], 1))
        total = part if total is None else total + part
    probs = jnp.exp2((tail - tails) * SCALE).astype(BF16)
    values = jnp.concatenate([jnp.where(m[:extra], vt, none) for m in masks], 0)
    total = total + dot(probs, jnp.concatenate([values, tail_ones], 1))
    return total[:, :C] / total[:, C:]


def gelu(v):
    inner = v * (GELU_A + GELU_B * (v * v))
    half = 0.5 * v
    return half * jnp.tanh(inner) + half


CHIPS = (
    (2, 2), (2, 1), (1, 2), (2, 3), (3, 2), (1, 1), (3, 3), (1, 3), (3, 1), (2, 0), (0, 2),
    (0, 1), (0, 3), (1, 0), (3, 0), (0, 0),
)


def chip_at(me, dy, dx):
    x, y = lax.rem(me // 2, 4), me // 8
    return (lax.rem(y + dy, 4) * 4 + lax.rem(x + dx, 4)) * 2


def kernel(
    counts_ref, shifts_ref, x_ref, gcol_hbm, wcq_hbm, wco_hbm, gwin_hbm, wwq_hbm, wwo_hbm,
    gmlp_hbm, wup_hbm, wdn_hbm, out_ref,
    gcol_ref, wcq_ref, wco_ref, gwin_ref, wwq_ref, wwo_ref, gmlp_ref, wup_ref, wdn_ref,
    rowoff, starts, xin, big, sendbuf, recv, r32, xl, srow, after, hsend, hrecv, wtok, attd, back,
    mask, blk, msg, got,
    x_sem, w_sem, in_send, in_recv, h_send, h_recv, b_send, b_recv, o_send, o_recv,
):
    me = lax.axis_index("lev")
    z = lax.axis_index("lon")
    east = lax.rem(z + 1, 8)
    west = lax.rem(z + 7, 8)

    barrier = pltpu.get_barrier_semaphore()

    def x_copy(slot):
        part = pl.ds(slot * LON, LON)
        return pltpu.make_async_copy(x_ref.at[part], xin.at[part], x_sem.at[slot])

    for slot in range(SLOTS):
        x_copy(slot).start()
    weights = [
        pltpu.make_async_copy(far, near, w_sem.at[n])
        for n, (far, near) in enumerate([
            (gcol_hbm, gcol_ref), (wcq_hbm, wcq_ref), (wco_hbm, wco_ref), (gwin_hbm, gwin_ref),
            (wwq_hbm, wwq_ref), (wwo_hbm, wwo_ref), (gmlp_hbm, gmlp_ref), (wup_hbm, wup_ref),
            (wdn_hbm, wdn_ref),
        ])
    ]

    def greet(step, _):
        pl.semaphore_signal(barrier, inc=1, device_id={"lev": lax.rem(me + step, LEVD)}, device_id_type=MESH)
        return 0

    lax.fori_loop(1, LEVD, greet, 0)
    for side in (east, west):
        pl.semaphore_signal(barrier, inc=1, device_id={"lon": side}, device_id_type=MESH)

    def widen(n, _):
        big[pl.ds(pl.multiple_of(n * LATS, LATS), LATS), :] = xin[n].astype(F32)
        return 0

    for slot in range(SLOTS):
        x_copy(slot).wait()
        lax.fori_loop(slot * LON, (slot + 1) * LON, widen, 0)
    pl.semaphore_wait(barrier, LEVD - 1 + 2)

    def in_copy(i, dest):
        return pltpu.make_async_remote_copy(
            src_ref=sendbuf.at[i, dest], dst_ref=recv.at[i, me],
            send_sem=in_send.at[i], recv_sem=in_recv.at[i],
            device_id={"lev": dest}, device_id_type=MESH,
        )

    core = lax.rem(me, 2)
    mate = me + 1 - 2 * core

    def send_to(i, dest):
        sendbuf[i, dest] = big[pl.ds(dest * LAT + i, ROWS_IN, stride=LATS), :].astype(BF16)
        in_copy(i, dest).start()

    def send_chunk(i, _, turn):
        for dy, dx in CHIPS[:-1]:
            send_to(i, chip_at(me, dy, dx) + turn)

        @pl.when(core != turn)
        def _():
            send_to(i, mate)

        return 0

    def keep_chunk(i, _):
        recv[i, me] = big[pl.ds(me * LAT + i, ROWS_IN, stride=LATS), :].astype(BF16)
        return 0

    lax.fori_loop(0, LAT, functools.partial(send_chunk, turn=0), 0)

    lax.fori_loop(0, LAT, functools.partial(send_chunk, turn=1), 0)

    lax.fori_loop(0, LAT, keep_chunk, 0)

    for weight in weights:
        weight.start()

    def place(level, carry):
        slab, slot = carry
        rowoff[level] = jnp.minimum(slab, LEVD - 1) * ROWS_IN + jnp.minimum(slot, SLOTS - 1) * LON
        more = slot + 1
        ends = more >= counts_ref[jnp.minimum(slab, LEVD - 1)]
        return jnp.where(ends, slab + 1, slab), jnp.where(ends, 0, more)

    lax.fori_loop(0, LEV, place, (jnp.int32(0), jnp.int32(0)))

    def begin(slab, start):
        starts[slab] = jnp.minimum(start, LEV - 1)
        return start + counts_ref[slab]

    lax.fori_loop(0, LEVD, begin, jnp.int32(0))

    def shift_rows(level, _):
        srow[pl.ds(level, 1), :] = jnp.full((1, C), shifts_ref[level // 2], jnp.int32)
        return 0

    lax.fori_loop(0, LEV, shift_rows, 0)

    row = lax.broadcasted_iota(jnp.int32, (PAIR, C), 0)

    def own_rows(p, _):
        shift = jnp.where(row < PAIR // 2, shifts_ref[2 * p], shifts_ref[2 * p + 1])
        for half in range(2):
            own = (lax.rem(row, HALF) + half * HALF >= shift) == (shift <= HALF)
            mask[half, pl.ds(pl.multiple_of(p * PAIR, PAIR), PAIR), :] = own.astype(jnp.int32)
        return 0

    lax.fori_loop(0, PAIRS, own_rows, 0)

    def halo_copy(i, half, side):
        return pltpu.make_async_remote_copy(
            src_ref=hsend.at[i, half], dst_ref=hrecv.at[i, half],
            send_sem=h_send.at[i, half], recv_sem=h_recv.at[i, half],
            device_id={"lon": side}, device_id_type=MESH,
        )

    masks64 = head_masks(LEV)
    ones64 = jnp.concatenate([m.astype(BF16) for m in masks64], 0)

    def column_chunk(i, _):
        pltpu.make_async_copy(
            recv.at[i, pl.ds(0, LEVD - 1)], recv.at[i, pl.ds(0, LEVD - 1)], in_recv.at[i]
        ).wait()

        def widen_in(d, _):
            r32[pl.ds(pl.multiple_of(d * ROWS_IN, ROWS_IN), ROWS_IN), :] = recv[i, d].astype(F32)
            return 0

        lax.fori_loop(0, LEVD, widen_in, 0, unroll=4)

        def pick(level, _):
            xl[pl.ds(pl.multiple_of(level * 16, 16), 16), :] = r32[pl.ds(rowoff[level], 16), :]
            return 0

        lax.fori_loop(0, LEV, pick, 0, unroll=16)

        cols = jnp.concatenate([xl[pl.ds(lon, LEV, stride=16), :] for lon in range(LON)], 0)
        packed = dot(norm(cols, gcol_ref[...]), wcq_ref[...]).astype(BF16)
        parts = []
        for n in range(LON):
            one = packed[n * LEV:(n + 1) * LEV]
            parts.append(attend_short(one[:, :C], one[:, C:2 * C], one[:, 2 * C:], masks64, ones64))
        done = cols + dot(jnp.concatenate(parts, 0).astype(BF16), wco_ref[...])
        normed = norm(done, gwin_ref[...])
        for half in range(2):
            for n in range(HALF):
                part = slice((half * HALF + n) * LEV, (half * HALF + n + 1) * LEV)
                after[pl.ds(half * HROWS + i * HALF + n, LEV, stride=COLS), :] = done[part]
                hsend[i, half, pl.ds(n * LEV, LEV), :] = normed[part]
            halo_copy(i, half, west if half == 0 else east).start()
        return 0

    def merge_chunk(i, _):
        for half in range(2):
            halo_copy(i, half, west if half == 0 else east).wait_recv()
            for n in range(HALF):
                lon = half * HALF + n
                shift = srow[...]
                own = (lon >= shift) == (shift <= HALF)
                mine = hsend[i, half, pl.ds(n * LEV, LEV), :].astype(F32)
                other = hrecv[i, half, pl.ds(n * LEV, LEV), :].astype(F32)
                at = half * HROWS + i * HALF + n
                wtok[pl.ds(at, LEV, stride=COLS), :] = jnp.where(own, mine, other)
        return 0

    for weight in weights:
        weight.wait()
    lax.fori_loop(0, LAT, column_chunk, 0)
    lax.fori_loop(0, LAT, merge_chunk, 0)

    masks144 = head_masks(PAIR)

    def back_copy(g, half, side):
        part = pl.ds(pl.multiple_of(g * (GROUP * PAIR), GROUP * PAIR), GROUP * PAIR)
        return pltpu.make_async_remote_copy(
            src_ref=attd.at[half, part], dst_ref=back.at[half, part],
            send_sem=b_send.at[half, g], recv_sem=b_recv.at[half, g],
            device_id={"lon": side}, device_id_type=MESH,
        )

    def window_pair(p, _):
        rows = WIN * PAIR
        at = pl.multiple_of(p * rows, rows)
        quarters = []
        for band in range(2 * WIN):
            for half in range(2):
                quarters.append(wtok[pl.ds(at + half * HROWS + band * (PAIR // 2), PAIR // 2), :])
        tokens = jnp.concatenate(quarters, 0).astype(BF16)
        packed = dot(tokens, wwq_ref[...]).astype(BF16)
        bands = []
        for band in range(2 * WIN):
            one = packed[band * PAIR:(band + 1) * PAIR]
            bands.append(attend(one[:, :C], one[:, C:2 * C], one[:, 2 * C:], masks144))
        for half in range(2):
            part = slice(half * (PAIR // 2), (half + 1) * (PAIR // 2))
            attd[half, pl.ds(at, rows), :] = jnp.concatenate([b[part] for b in bands], 0).astype(BF16)
        return 0

    def window_group(g, _):
        lax.fori_loop(g * (GROUP // WIN), (g + 1) * (GROUP // WIN), window_pair, 0)
        back_copy(g, 0, east).start()
        back_copy(g, 1, west).start()
        return 0

    lax.fori_loop(0, GROUPS, window_group, 0)

    def out_copy(half, dest):
        return pltpu.make_async_remote_copy(
            src_ref=msg.at[half, dest], dst_ref=got.at[half, me],
            send_sem=o_send.at[half], recv_sem=o_recv.at[half],
            device_id={"lev": dest}, device_id_type=MESH,
        )

    for half in range(2):

        def feed_pair(p, _):
            rows = FEED * PAIR
            at = pl.multiple_of(p * rows, rows)
            attended = jnp.where(
                mask[half, pl.ds(at, rows), :] > 0,
                attd[half, pl.ds(at, rows), :].astype(F32),
                back[half, pl.ds(at, rows), :].astype(F32),
            ).astype(BF16)
            stay = after[pl.ds(at + half * HROWS, rows), :] + dot(attended, wwo_ref[...])
            hidden = gelu(dot(norm(stay, gmlp_ref[...]), wup_ref[...]))
            blk[half, pl.ds(at, rows), :] = stay + dot(hidden.astype(BF16), wdn_ref[...])
            return 0

        def feed_group(g, _):
            back_copy(g, half, east if half == 0 else west).wait_recv()
            lax.fori_loop(g * (GROUP // FEED), (g + 1) * (GROUP // FEED), feed_pair, 0)
            return 0

        blk[half, pl.ds(HROWS, PAIR), :] = jnp.zeros((PAIR, C), F32)
        lax.fori_loop(0, GROUPS, feed_group, 0)

        def block_for(dest):
            rows = blk[half, pl.ds(starts[dest] * COLS, ROWS_OUT), :]
            return jnp.where(row < counts_ref[dest] * COLS, rows, 0.0).astype(BF16)

        def fill(dest, _):
            msg[half, dest] = block_for(dest)
            return 0

        lax.fori_loop(0, LEVD, fill, 0)
        for dy, dx in CHIPS[:-1]:
            for turn in range(2):
                out_copy(half, chip_at(me, dy, dx) + turn).start()
        out_copy(half, mate).start()
        got[half, me] = msg[half, me]

    for half in range(2):
        pltpu.make_async_copy(
            got.at[half, pl.ds(0, LEVD - 1)], got.at[half, pl.ds(0, LEVD - 1)], o_recv.at[half]
        ).wait()

        def widen_out(e, _):
            big[pl.ds(pl.multiple_of(e * ROWS_OUT, ROWS_OUT), ROWS_OUT), :] = got[half, e].astype(F32)
            return 0

        lax.fori_loop(0, LEVD, widen_out, 0)

        def unpack(n, _):
            slot, lon = n // HALF, lax.rem(n, HALF)
            for i in range(LAT):
                r32[pl.ds(i, LEVD, stride=LAT), :] = big[
                    pl.ds(slot * COLS + i * HALF + lon, LEVD, stride=ROWS_OUT), :
                ]
            at = slot * LON + half * HALF + lon
            out_ref[at] = r32[pl.ds(0, LATS), :].astype(BF16)
            return 0

        lax.fori_loop(0, SLOTS * HALF, unpack, 0)

    for i in range(LAT):
        pltpu.make_async_copy(
            sendbuf.at[i, pl.ds(0, LEVD - 1)], sendbuf.at[i, pl.ds(0, LEVD - 1)], in_send.at[i]
        ).wait()
        halo_copy(i, 0, west).wait_send()
        halo_copy(i, 1, east).wait_send()
    for g in range(GROUPS):
        back_copy(g, 0, east).wait_send()
        back_copy(g, 1, west).wait_send()
    for half in range(2):
        pltpu.make_async_copy(
            msg.at[half, pl.ds(0, LEVD - 1)], msg.at[half, pl.ds(0, LEVD - 1)], o_send.at[half]
        ).wait()


def per_device(
    levels_in, slab_levels, shifts, gain_col, w_col_qkv, w_col_out, gain_win, w_win_qkv, w_win_out,
    gain_mlp, w_up, w_down,
):
    x = levels_in.transpose(0, 2, 1, 3).reshape(ROWS_IN, LATS, C)
    weights = [
        gain_col.reshape(1, C), w_col_qkv, w_col_out, gain_win.reshape(1, C), w_win_qkv, w_win_out,
        gain_mlp.reshape(1, C), w_up, w_down,
    ]
    smem = pl.BlockSpec(memory_space=pltpu.SMEM)
    vmem = pl.BlockSpec(memory_space=pltpu.VMEM)
    dma = pltpu.SemaphoreType.DMA
    out = pl.pallas_call(
        kernel,
        out_shape=pltpu.VMEM((ROWS_IN, LATS, C), BF16),
        in_specs=[smem, smem] + [pl.BlockSpec(memory_space=pl.ANY)] * 10,
        out_specs=vmem,
        scratch_shapes=[
            *[pltpu.VMEM(w.shape, w.dtype) for w in weights],
            pltpu.SMEM((LEV,), jnp.int32),
            pltpu.SMEM((LEVD,), jnp.int32),
            pltpu.VMEM((ROWS_IN, LATS, C), BF16),
            pltpu.VMEM((ROWS_IN * LATS, C), F32),
            pltpu.VMEM((LAT, LEVD, ROWS_IN, C), BF16),
            pltpu.VMEM((LAT, LEVD, ROWS_IN, C), BF16),
            pltpu.VMEM((LEVD * ROWS_IN + 8, C), F32),
            pltpu.VMEM((LEV * 16, C), F32),
            pltpu.VMEM((LEV, C), jnp.int32),
            pltpu.VMEM((2 * HROWS, C), F32),
            pltpu.VMEM((LAT, 2, HCOL, C), BF16),
            pltpu.VMEM((LAT, 2, HCOL, C), BF16),
            pltpu.VMEM((2 * HROWS, C), F32),
            pltpu.VMEM((2, HROWS, C), BF16),
            pltpu.VMEM((2, HROWS, C), BF16),
            pltpu.VMEM((2, HROWS, C), jnp.int32),
            pltpu.VMEM((2, HROWS + PAIR, C), F32),
            pltpu.VMEM((2, LEVD, ROWS_OUT, C), BF16),
            pltpu.VMEM((2, LEVD, ROWS_OUT, C), BF16),
            dma((SLOTS,)), dma((9,)),
            dma((LAT,)), dma((LAT,)),
            dma((LAT, 2)), dma((LAT, 2)),
            dma((2, GROUPS)), dma((2, GROUPS)),
            dma((2,)), dma((2,)),
        ],
        compiler_params=pltpu.CompilerParams(
            collective_id=0, has_side_effects=True, vmem_limit_bytes=56 * 1024 * 1024
        ),
    )(slab_levels, shifts, x, *weights)
    return out.reshape(SLOTS, LON, LATS, C).transpose(0, 2, 1, 3)


def solution(mesh):
    placed = (P("lev", None, "lon", None),) + (P(),) * 11
    return jax.shard_map(
        per_device,
        mesh=mesh,
        in_specs=placed,
        out_specs=P("lev", None, "lon", None),
        check_vma=False,
    )
```

```python
import functools
import math

import jax
import jax.numpy as jnp
from jax import lax
from jax.experimental import pallas as pl
from jax.experimental.pallas import tpu as pltpu
from jax.sharding import PartitionSpec as P

HEADS = 4
EPS = 1e-05
MESH = pl.DeviceIdType.MESH
F32 = jnp.float32
BF16 = jnp.bfloat16

SLOTS = 4
LON = 12
LAT = 6
HALF = LON // 2
LEVD = 32
LEV = 64
LATS = LAT * LEVD
C = 128
SUBS = 3
PART = HALF * LAT // SUBS
PARTS = 2 * SUBS
ROWS_IN = SLOTS * LON
ROWS_OUT = SLOTS * PART
PROWS = LEV * PART
BAND = 2 * PART
SEQ = PARTS * BAND
BANDS = LEV // 2
GROUPS = 4
GROUP = BANDS // GROUPS
GROWS = GROUP * BAND
HCOL = HALF * LEV
GELU_A = math.sqrt(2.0 / math.pi)
GELU_B = GELU_A * 0.044715
SCALE = math.log2(math.e) / math.sqrt(C // HEADS)


def norm(v, gain):
    centred = v - jnp.mean(v, -1, keepdims=True)
    spread = jnp.mean(centred * centred, -1, keepdims=True)
    return (centred * lax.rsqrt(spread + EPS) * gain).astype(BF16)


def dot(a, b):
    return jnp.dot(a, b, preferred_element_type=F32)


def dot_nt(a, b):
    return lax.dot_general(a, b, (((1,), (1,)), ((), ())), preferred_element_type=F32)


def head_masks(rows):
    lane = lax.broadcasted_iota(jnp.int32, (rows, C), 1)
    return [(lane // (C // HEADS)) == h for h in range(HEADS)]


def attend(q, k, v, masks):
    n = q.shape[0]
    value = jnp.concatenate([v, jnp.ones((n, C), BF16)], 1)
    over, under = None, None
    for h in range(HEADS):
        scores = dot_nt(jnp.where(masks[h], q, jnp.zeros_like(q)), k)
        top = jnp.max(scores, -1, keepdims=True)
        probs = jnp.exp2((scores - top) * SCALE).astype(BF16)
        both = dot(probs, value)
        over = both[:, :C] if h == 0 else jnp.where(masks[h], both[:, :C], over)
        under = both[:, C:] if h == 0 else jnp.where(masks[h], both[:, C:], under)
    return over / under


def attend_short(q, k, v, masks, ones):
    zero = jnp.zeros_like(k)
    keys = jnp.concatenate([jnp.where(m, k, zero) for m in masks], 0)
    values = jnp.concatenate([jnp.where(m, v, zero) for m in masks], 0)
    scores = dot_nt(q, keys)
    low = lax.broadcasted_iota(jnp.int32, (LEV, C), 1) < LEV
    probs = []
    for t in range(2):
        part = scores[:, t * C:(t + 1) * C]
        top = jnp.where(
            low,
            jnp.max(jnp.where(low, part, -jnp.inf), -1, keepdims=True),
            jnp.max(jnp.where(low, -jnp.inf, part), -1, keepdims=True),
        )
        probs.append(jnp.exp2((part - top) * SCALE).astype(BF16))
    both = dot(jnp.concatenate(probs, 1), jnp.concatenate([values, ones], 1))
    return both[:, :C] / both[:, C:]


def attend_long(q, k, v, masks, tail_masks, ones, tail_ones):
    n = q.shape[0]
    extra = n - C
    km, kt, vm, vt = k[:C], k[C:], v[:C], v[C:]
    zero, none = jnp.zeros_like(km), jnp.zeros_like(kt)
    tail = dot_nt(q, jnp.concatenate([jnp.where(m[:extra], kt, none) for m in masks], 0))
    tails = jnp.zeros((n, HEADS * extra), F32)
    total = None
    for h in range(HEADS):
        scores = dot_nt(q, jnp.where(masks[h], km, zero))
        mine = jnp.where(tail_masks[h], tail, -jnp.inf)
        top = jnp.max(jnp.maximum(scores, jnp.concatenate([mine, jnp.full((n, C - HEADS * extra), -jnp.inf, F32)], 1)), -1, keepdims=True)
        probs = jnp.exp2((scores - top) * SCALE).astype(BF16)
        tails = jnp.where(tail_masks[h], top, tails)
        part = dot(probs, jnp.concatenate([jnp.where(masks[h], vm, zero), ones[h]], 1))
        total = part if total is None else total + part
    probs = jnp.exp2((tail - tails) * SCALE).astype(BF16)
    values = jnp.concatenate([jnp.where(m[:extra], vt, none) for m in masks], 0)
    total = total + dot(probs, jnp.concatenate([values, tail_ones], 1))
    return total[:, :C] / total[:, C:]


def gelu(v):
    inner = v * (GELU_A + GELU_B * (v * v))
    half = 0.5 * v
    return half * jnp.tanh(inner) + half


CHIPS = (
    (2, 2), (2, 1), (1, 2), (2, 3), (3, 2), (1, 1), (3, 3), (1, 3), (3, 1), (2, 0), (0, 2),
    (0, 1), (0, 3), (1, 0), (3, 0), (0, 0),
)


def chip_at(me, dy, dx):
    x, y = lax.rem(me // 2, 4), me // 8
    return (lax.rem(y + dy, 4) * 4 + lax.rem(x + dx, 4)) * 2


def kernel(
    counts_ref, shifts_ref, x_ref, gcol_hbm, wcq_hbm, wco_hbm, gwin_hbm, wwq_hbm, wwo_hbm,
    gmlp_hbm, wup_hbm, wdn_hbm, out_ref,
    gcol_ref, wcq_ref, wco_ref, gwin_ref, wwq_ref, wwo_ref, gmlp_ref, wup_ref, wdn_ref,
    rowoff, starts, xin, big, sendbuf, recv, r32, xl, srow, after, hsend, hrecv, wtok, attd, back,
    mask, blk, msg, got,
    x_sem, w_sem, in_send, in_recv, h_send, h_recv, b_send, b_recv, o_send, o_recv,
):
    me = lax.axis_index("lev")
    z = lax.axis_index("lon")
    east = lax.rem(z + 1, 8)
    west = lax.rem(z + 7, 8)

    barrier = pltpu.get_barrier_semaphore()

    def x_copy(slot):
        part = pl.ds(slot * LON, LON)
        return pltpu.make_async_copy(x_ref.at[part], xin.at[part], x_sem.at[slot])

    for slot in range(SLOTS):
        x_copy(slot).start()
    weights = [
        pltpu.make_async_copy(far, near, w_sem.at[n])
        for n, (far, near) in enumerate([
            (gcol_hbm, gcol_ref), (wcq_hbm, wcq_ref), (wco_hbm, wco_ref), (gwin_hbm, gwin_ref),
            (wwq_hbm, wwq_ref), (wwo_hbm, wwo_ref), (gmlp_hbm, gmlp_ref), (wup_hbm, wup_ref),
            (wdn_hbm, wdn_ref),
        ])
    ]

    def greet(step, _):
        pl.semaphore_signal(barrier, inc=1, device_id={"lev": lax.rem(me + step, LEVD)}, device_id_type=MESH)
        return 0

    lax.fori_loop(1, LEVD, greet, 0)
    for side in (east, west):
        pl.semaphore_signal(barrier, inc=1, device_id={"lon": side}, device_id_type=MESH)

    def widen(n, _):
        big[pl.ds(pl.multiple_of(n * LATS, LATS), LATS), :] = xin[n].astype(F32)
        return 0

    for slot in range(SLOTS):
        x_copy(slot).wait()
        lax.fori_loop(slot * LON, (slot + 1) * LON, widen, 0)
    pl.semaphore_wait(barrier, LEVD - 1 + 2)

    def in_copy(i, dest):
        return pltpu.make_async_remote_copy(
            src_ref=sendbuf.at[i, dest], dst_ref=recv.at[i, me],
            send_sem=in_send.at[i], recv_sem=in_recv.at[i],
            device_id={"lev": dest}, device_id_type=MESH,
        )

    core = lax.rem(me, 2)
    mate = me + 1 - 2 * core

    def send_to(i, dest):
        sendbuf[i, dest] = big[pl.ds(dest * LAT + i, ROWS_IN, stride=LATS), :].astype(BF16)
        in_copy(i, dest).start()

    def send_chunk(i, _, turn):
        for dy, dx in CHIPS[:-1]:
            send_to(i, chip_at(me, dy, dx) + turn)

        @pl.when(core != turn)
        def _():
            send_to(i, mate)

        return 0

    def keep_chunk(i, _):
        recv[i, me] = big[pl.ds(me * LAT + i, ROWS_IN, stride=LATS), :].astype(BF16)
        return 0

    lax.fori_loop(0, LAT, functools.partial(send_chunk, turn=0), 0)

    lax.fori_loop(0, LAT, functools.partial(send_chunk, turn=1), 0)

    lax.fori_loop(0, LAT, keep_chunk, 0)

    for weight in weights:
        weight.start()

    def place(level, carry):
        slab, slot = carry
        rowoff[level] = jnp.minimum(slab, LEVD - 1) * ROWS_IN + jnp.minimum(slot, SLOTS - 1) * LON
        more = slot + 1
        ends = more >= counts_ref[jnp.minimum(slab, LEVD - 1)]
        return jnp.where(ends, slab + 1, slab), jnp.where(ends, 0, more)

    lax.fori_loop(0, LEV, place, (jnp.int32(0), jnp.int32(0)))

    def begin(slab, start):
        starts[slab] = jnp.minimum(start, LEV - 1)
        return start + counts_ref[slab]

    lax.fori_loop(0, LEVD, begin, jnp.int32(0))

    def shift_rows(level, _):
        srow[pl.ds(level, 1), :] = jnp.full((1, C), shifts_ref[level // 2], jnp.int32)
        return 0

    lax.fori_loop(0, LEV, shift_rows, 0)

    row = lax.broadcasted_iota(jnp.int32, (2 * BAND, C), 0)

    def own_rows(p, _):
        shift = jnp.where(row < BAND, shifts_ref[2 * p], shifts_ref[2 * p + 1])
        for half in range(2):
            own = (lax.rem(row, HALF) + half * HALF >= shift) == (shift <= HALF)
            mask[half, pl.ds(pl.multiple_of(p * 2 * BAND, 2 * BAND), 2 * BAND), :] = own.astype(jnp.int32)
        return 0

    lax.fori_loop(0, BANDS // 2, own_rows, 0)

    def halo_copy(i, half, side):
        return pltpu.make_async_remote_copy(
            src_ref=hsend.at[i, half], dst_ref=hrecv.at[i, half],
            send_sem=h_send.at[i, half], recv_sem=h_recv.at[i, half],
            device_id={"lon": side}, device_id_type=MESH,
        )

    def column_at(i, half, n):
        return (half * SUBS + i // 2) * PROWS + lax.rem(i, 2) * HALF + n

    masks64 = head_masks(LEV)
    ones64 = jnp.concatenate([m.astype(BF16) for m in masks64], 0)

    def column_chunk(i, _):
        pltpu.make_async_copy(
            recv.at[i, pl.ds(0, LEVD - 1)], recv.at[i, pl.ds(0, LEVD - 1)], in_recv.at[i]
        ).wait()

        def widen_in(d, _):
            r32[pl.ds(pl.multiple_of(d * ROWS_IN, ROWS_IN), ROWS_IN), :] = recv[i, d].astype(F32)
            return 0

        lax.fori_loop(0, LEVD, widen_in, 0, unroll=4)

        def pick(level, _):
            xl[pl.ds(pl.multiple_of(level * 16, 16), 16), :] = r32[pl.ds(rowoff[level], 16), :]
            return 0

        lax.fori_loop(0, LEV, pick, 0, unroll=16)

        cols = jnp.concatenate([xl[pl.ds(lon, LEV, stride=16), :] for lon in range(LON)], 0)
        packed = dot(norm(cols, gcol_ref[...]), wcq_ref[...]).astype(BF16)
        parts = []
        for n in range(LON):
            one = packed[n * LEV:(n + 1) * LEV]
            parts.append(attend_short(one[:, :C], one[:, C:2 * C], one[:, 2 * C:], masks64, ones64))
        done = cols + dot(jnp.concatenate(parts, 0).astype(BF16), wco_ref[...])
        normed = norm(done, gwin_ref[...])
        for half in range(2):
            for n in range(HALF):
                part = slice((half * HALF + n) * LEV, (half * HALF + n + 1) * LEV)
                after[pl.ds(column_at(i, half, n), LEV, stride=PART), :] = done[part]
                hsend[i, half, pl.ds(n * LEV, LEV), :] = normed[part]
            halo_copy(i, half, west if half == 0 else east).start()
        return 0

    def merge_chunk(i, _):
        for half in range(2):
            halo_copy(i, half, west if half == 0 else east).wait_recv()
            for n in range(HALF):
                lon = half * HALF + n
                shift = srow[...]
                own = (lon >= shift) == (shift <= HALF)
                mine = hsend[i, half, pl.ds(n * LEV, LEV), :].astype(F32)
                other = hrecv[i, half, pl.ds(n * LEV, LEV), :].astype(F32)
                wtok[pl.ds(column_at(i, half, n), LEV, stride=PART), :] = jnp.where(own, mine, other)
        return 0

    for weight in weights:
        weight.wait()
    lax.fori_loop(0, LAT, column_chunk, 0)
    lax.fori_loop(0, LAT, merge_chunk, 0)

    masks_seq = head_masks(SEQ)

    def back_copy(g, half, side):
        parts = pl.ds(half * SUBS, SUBS)
        rows = pl.ds(pl.multiple_of(g * GROWS, GROWS), GROWS)
        return pltpu.make_async_remote_copy(
            src_ref=attd.at[parts, rows], dst_ref=back.at[parts, rows],
            send_sem=b_send.at[half, g], recv_sem=b_recv.at[half, g],
            device_id={"lon": side}, device_id_type=MESH,
        )

    def window_group(g, _):
        at = pl.multiple_of(g * GROWS, GROWS)
        pieces = []
        for band in range(GROUP):
            for part in range(PARTS):
                pieces.append(wtok[pl.ds(part * PROWS + at + band * BAND, BAND), :])
        tokens = jnp.concatenate(pieces, 0).astype(BF16)
        packed = dot(tokens, wwq_ref[...]).astype(BF16)
        bands = []
        for band in range(GROUP):
            one = packed[band * SEQ:(band + 1) * SEQ]
            bands.append(attend(one[:, :C], one[:, C:2 * C], one[:, 2 * C:], masks_seq))
        for part in range(PARTS):
            rows = slice(part * BAND, (part + 1) * BAND)
            attd[part, pl.ds(at, GROWS), :] = jnp.concatenate([b[rows] for b in bands], 0).astype(BF16)
        back_copy(g, 0, east).start()
        back_copy(g, 1, west).start()
        return 0

    lax.fori_loop(0, GROUPS, window_group, 0)

    def out_copy(part, dest):
        return pltpu.make_async_remote_copy(
            src_ref=msg.at[part, dest], dst_ref=got.at[part, me],
            send_sem=o_send.at[part], recv_sem=o_recv.at[part],
            device_id={"lev": dest}, device_id_type=MESH,
        )

    def feed_part(part, _):
        half = part // SUBS
        attended = jnp.where(
            mask[half] > 0, attd[part].astype(F32), back[part].astype(F32)
        ).astype(BF16)
        stay = after[pl.ds(pl.multiple_of(part * PROWS, PROWS), PROWS), :] + dot(attended, wwo_ref[...])
        hidden = gelu(dot(norm(stay, gmlp_ref[...]), wup_ref[...]))
        blk[pl.ds(0, PROWS), :] = stay + dot(hidden.astype(BF16), wdn_ref[...])

        def fill(dest, _):
            rows = blk[pl.ds(starts[dest] * PART, ROWS_OUT), :]
            msg[part, dest] = jnp.where(row < counts_ref[dest] * PART, rows, 0.0).astype(BF16)
            return 0

        lax.fori_loop(0, LEVD, fill, 0)
        for dy, dx in CHIPS[:-1]:
            for turn in range(2):
                out_copy(part, chip_at(me, dy, dx) + turn).start()
        out_copy(part, mate).start()
        got[part, me] = msg[part, me]
        return 0

    blk[pl.ds(PROWS, ROWS_OUT), :] = jnp.zeros((ROWS_OUT, C), F32)
    for half in range(2):
        for g in range(GROUPS):
            back_copy(g, half, east if half == 0 else west).wait_recv()
        lax.fori_loop(half * SUBS, (half + 1) * SUBS, feed_part, 0)

    stage = LEVD * ROWS_OUT

    def take_part(part, _):
        pltpu.make_async_copy(
            got.at[part, pl.ds(0, LEVD - 1)], got.at[part, pl.ds(0, LEVD - 1)], o_recv.at[part]
        ).wait()

        def widen_out(e, _):
            big[pl.ds(pl.multiple_of(e * ROWS_OUT, ROWS_OUT), ROWS_OUT), :] = got[part, e].astype(F32)
            return 0

        lax.fori_loop(0, LEVD, widen_out, 0, unroll=4)

        def sort(n, _):
            slot, lon = n // HALF, lax.rem(n, HALF)
            for i in range(2):
                big[pl.ds(stage + n * LATS + lax.rem(part, SUBS) * 2 + i, LEVD, stride=LAT), :] = big[
                    pl.ds(slot * PART + i * HALF + lon, LEVD, stride=ROWS_OUT), :
                ]
            return 0

        lax.fori_loop(0, SLOTS * HALF, sort, 0, unroll=4)
        return 0

    for half in range(2):
        lax.fori_loop(half * SUBS, (half + 1) * SUBS, take_part, 0)

        def give(n, _):
            slot, lon = n // HALF, lax.rem(n, HALF)
            rows = big[pl.ds(pl.multiple_of(stage + n * LATS, LATS), LATS), :]
            out_ref[slot * LON + half * HALF + lon] = rows.astype(BF16)
            return 0

        lax.fori_loop(0, SLOTS * HALF, give, 0, unroll=4)

    for i in range(LAT):
        pltpu.make_async_copy(
            sendbuf.at[i, pl.ds(0, LEVD - 1)], sendbuf.at[i, pl.ds(0, LEVD - 1)], in_send.at[i]
        ).wait()
        halo_copy(i, 0, west).wait_send()
        halo_copy(i, 1, east).wait_send()
    for g in range(GROUPS):
        back_copy(g, 0, east).wait_send()
        back_copy(g, 1, west).wait_send()
    for part in range(PARTS):
        pltpu.make_async_copy(
            msg.at[part, pl.ds(0, LEVD - 1)], msg.at[part, pl.ds(0, LEVD - 1)], o_send.at[part]
        ).wait()


def per_device(
    levels_in, slab_levels, shifts, gain_col, w_col_qkv, w_col_out, gain_win, w_win_qkv, w_win_out,
    gain_mlp, w_up, w_down,
):
    x = levels_in.transpose(0, 2, 1, 3).reshape(ROWS_IN, LATS, C)
    weights = [
        gain_col.reshape(1, C), w_col_qkv, w_col_out, gain_win.reshape(1, C), w_win_qkv, w_win_out,
        gain_mlp.reshape(1, C), w_up, w_down,
    ]
    smem = pl.BlockSpec(memory_space=pltpu.SMEM)
    vmem = pl.BlockSpec(memory_space=pltpu.VMEM)
    dma = pltpu.SemaphoreType.DMA
    out = pl.pallas_call(
        kernel,
        out_shape=pltpu.VMEM((ROWS_IN, LATS, C), BF16),
        in_specs=[smem, smem] + [pl.BlockSpec(memory_space=pl.ANY)] * 10,
        out_specs=vmem,
        scratch_shapes=[
            *[pltpu.VMEM(w.shape, w.dtype) for w in weights],
            pltpu.SMEM((LEV,), jnp.int32),
            pltpu.SMEM((LEVD,), jnp.int32),
            pltpu.VMEM((ROWS_IN, LATS, C), BF16),
            pltpu.VMEM((ROWS_IN * LATS, C), F32),
            pltpu.VMEM((LAT, LEVD, ROWS_IN, C), BF16),
            pltpu.VMEM((LAT, LEVD, ROWS_IN, C), BF16),
            pltpu.VMEM((LEVD * ROWS_IN + 8, C), F32),
            pltpu.VMEM((LEV * 16, C), F32),
            pltpu.VMEM((LEV, C), jnp.int32),
            pltpu.VMEM((PARTS * PROWS, C), F32),
            pltpu.VMEM((LAT, 2, HCOL, C), BF16),
            pltpu.VMEM((LAT, 2, HCOL, C), BF16),
            pltpu.VMEM((PARTS * PROWS, C), F32),
            pltpu.VMEM((PARTS, PROWS, C), BF16),
            pltpu.VMEM((PARTS, PROWS, C), BF16),
            pltpu.VMEM((2, PROWS, C), jnp.int32),
            pltpu.VMEM((PROWS + ROWS_OUT, C), F32),
            pltpu.VMEM((PARTS, LEVD, ROWS_OUT, C), BF16),
            pltpu.VMEM((PARTS, LEVD, ROWS_OUT, C), BF16),
            dma((SLOTS,)), dma((9,)),
            dma((LAT,)), dma((LAT,)),
            dma((LAT, 2)), dma((LAT, 2)),
            dma((2, GROUPS)), dma((2, GROUPS)),
            dma((PARTS,)), dma((PARTS,)),
        ],
        compiler_params=pltpu.CompilerParams(
            collective_id=0, has_side_effects=True, vmem_limit_bytes=56 * 1024 * 1024
        ),
    )(slab_levels, shifts, x, *weights)
    return out.reshape(SLOTS, LON, LATS, C).transpose(0, 2, 1, 3)


def solution(mesh):
    placed = (P("lev", None, "lon", None),) + (P(),) * 11
    return jax.shard_map(
        per_device,
        mesh=mesh,
        in_specs=placed,
        out_specs=P("lev", None, "lon", None),
        check_vma=False,
    )
```

```python
import functools
import math

import jax
import jax.numpy as jnp
from jax import lax
from jax.experimental import pallas as pl
from jax.experimental.pallas import tpu as pltpu
from jax.sharding import PartitionSpec as P

HEADS = 4
EPS = 1e-05
MESH = pl.DeviceIdType.MESH
F32 = jnp.float32
BF16 = jnp.bfloat16

SLOTS = 4
LON = 12
LAT = 6
HALF = LON // 2
LEVD = 32
LEV = 64
LATS = LAT * LEVD
C = 128
SUBS = 3
PART = HALF * LAT // SUBS
PARTS = 2 * SUBS
ROWS_IN = SLOTS * LON
ROWS_OUT = SLOTS * PART
PROWS = LEV * PART
BAND = 2 * PART
SEQ = PARTS * BAND
BANDS = LEV // 2
GROUPS = 8
GROUP = BANDS // GROUPS
GROWS = GROUP * BAND
HCOL = HALF * LEV
GELU_A = math.sqrt(2.0 / math.pi)
GELU_B = GELU_A * 0.044715
SCALE = math.log2(math.e) / math.sqrt(C // HEADS)


def norm(v, gain):
    centred = v - jnp.mean(v, -1, keepdims=True)
    spread = jnp.mean(centred * centred, -1, keepdims=True)
    return (centred * lax.rsqrt(spread + EPS) * gain).astype(BF16)


def dot(a, b):
    return jnp.dot(a, b, preferred_element_type=F32)


def dot_nt(a, b):
    return lax.dot_general(a, b, (((1,), (1,)), ((), ())), preferred_element_type=F32)


def head_masks(rows):
    lane = lax.broadcasted_iota(jnp.int32, (rows, C), 1)
    return [(lane // (C // HEADS)) == h for h in range(HEADS)]


def attend_short(q, k, v, masks, ones):
    zero = jnp.zeros_like(k)
    keys = jnp.concatenate([jnp.where(m, k, zero) for m in masks], 0)
    values = jnp.concatenate([jnp.where(m, v, zero) for m in masks], 0)
    scores = dot_nt(q, keys)
    low = lax.broadcasted_iota(jnp.int32, (LEV, C), 1) < LEV
    probs = []
    for t in range(2):
        part = scores[:, t * C:(t + 1) * C]
        top = jnp.where(
            low,
            jnp.max(jnp.where(low, part, -jnp.inf), -1, keepdims=True),
            jnp.max(jnp.where(low, -jnp.inf, part), -1, keepdims=True),
        )
        probs.append(jnp.exp2((part - top) * SCALE).astype(BF16))
    both = dot(jnp.concatenate(probs, 1), jnp.concatenate([values, ones], 1))
    return both[:, :C] / both[:, C:]


def attend_long(q, k, v, masks, tail_masks, ones, tail_ones):
    extra = SEQ - C
    tail_of = [m[:extra] for m in masks]
    km, kt, vm, vt = k[:C], k[C:], v[:C], v[C:]
    zero, none = jnp.zeros_like(km), jnp.zeros_like(kt)
    pad = jnp.zeros((C - HEADS * extra, C), BF16)
    tail = dot_nt(q, jnp.concatenate([jnp.where(m, kt, none) for m in tail_of] + [pad], 0))
    tops, total = jnp.zeros((SEQ, C), F32), None
    for first in range(0, HEADS, 2):
        heads = (first, first + 1)
        scores = dot_nt(q, jnp.concatenate([jnp.where(masks[h], km, zero) for h in heads], 0))
        probs = []
        for n, h in enumerate(heads):
            mine = scores[:, n * C:(n + 1) * C]
            top = jnp.max(jnp.maximum(mine, jnp.where(tail_masks[h], tail, -jnp.inf)), -1, keepdims=True)
            probs.append(jnp.exp2((mine - top) * SCALE).astype(BF16))
            tops = jnp.where(tail_masks[h], top, tops)
        values = jnp.concatenate([jnp.where(masks[h], vm, zero) for h in heads], 0)
        part = dot(jnp.concatenate(probs, 1), jnp.concatenate([values, ones[first // 2]], 1))
        total = part if total is None else total + part
    probs = jnp.exp2((tail - tops) * SCALE).astype(BF16)
    values = jnp.concatenate([jnp.where(m, vt, none) for m in tail_of] + [pad], 0)
    total = total + dot(probs, jnp.concatenate([values, tail_ones], 1))
    return total[:, :C] / total[:, C:]


def gelu(v):
    inner = v * (GELU_A + GELU_B * (v * v))
    half = 0.5 * v
    return half * jnp.tanh(inner) + half


CHIPS = (
    (2, 2), (2, 1), (1, 2), (2, 3), (3, 2), (1, 1), (3, 3), (1, 3), (3, 1), (2, 0), (0, 2),
    (0, 1), (0, 3), (1, 0), (3, 0), (0, 0),
)


def chip_at(me, dy, dx):
    x, y = lax.rem(me // 2, 4), me // 8
    return (lax.rem(y + dy, 4) * 4 + lax.rem(x + dx, 4)) * 2


def kernel(
    counts_ref, shifts_ref, x_ref, gcol_hbm, wcq_hbm, wco_hbm, gwin_hbm, wwq_hbm, wwo_hbm,
    gmlp_hbm, wup_hbm, wdn_hbm, out_ref,
    gcol_ref, wcq_ref, wco_ref, gwin_ref, wwq_ref, wwo_ref, gmlp_ref, wup_ref, wdn_ref,
    rowoff, starts, xin, big, sendbuf, recv, r32, xl, srow, after, hsend, hrecv, wtok, attd, back,
    mask, blk, msg, got,
    x_sem, w_sem, in_send, in_recv, h_send, h_recv, b_send, b_recv, o_send, o_recv,
):
    me = lax.axis_index("lev")
    z = lax.axis_index("lon")
    east = lax.rem(z + 1, 8)
    west = lax.rem(z + 7, 8)

    barrier = pltpu.get_barrier_semaphore()

    def x_copy(slot):
        part = pl.ds(slot * LON, LON)
        return pltpu.make_async_copy(x_ref.at[part], xin.at[part], x_sem.at[slot])

    for slot in range(SLOTS):
        x_copy(slot).start()
    weights = [
        pltpu.make_async_copy(far, near, w_sem.at[n])
        for n, (far, near) in enumerate([
            (gcol_hbm, gcol_ref), (wcq_hbm, wcq_ref), (wco_hbm, wco_ref), (gwin_hbm, gwin_ref),
            (wwq_hbm, wwq_ref), (wwo_hbm, wwo_ref), (gmlp_hbm, gmlp_ref), (wup_hbm, wup_ref),
            (wdn_hbm, wdn_ref),
        ])
    ]

    def greet(step, _):
        pl.semaphore_signal(barrier, inc=1, device_id={"lev": lax.rem(me + step, LEVD)}, device_id_type=MESH)
        return 0

    lax.fori_loop(1, LEVD, greet, 0)
    for side in (east, west):
        pl.semaphore_signal(barrier, inc=1, device_id={"lon": side}, device_id_type=MESH)

    def widen(n, _):
        big[pl.ds(pl.multiple_of(n * LATS, LATS), LATS), :] = xin[n].astype(F32)
        return 0

    for slot in range(SLOTS):
        x_copy(slot).wait()
        lax.fori_loop(slot * LON, (slot + 1) * LON, widen, 0)
    pl.semaphore_wait(barrier, LEVD - 1 + 2)

    def in_copy(i, dest):
        return pltpu.make_async_remote_copy(
            src_ref=sendbuf.at[i, dest], dst_ref=recv.at[i, me],
            send_sem=in_send.at[i], recv_sem=in_recv.at[i],
            device_id={"lev": dest}, device_id_type=MESH,
        )

    core = lax.rem(me, 2)
    mate = me + 1 - 2 * core

    def send_to(i, dest):
        sendbuf[i, dest] = big[pl.ds(dest * LAT + i, ROWS_IN, stride=LATS), :].astype(BF16)
        in_copy(i, dest).start()

    def send_chunk(i, _, turn):
        for dy, dx in CHIPS[:-1]:
            send_to(i, chip_at(me, dy, dx) + turn)

        @pl.when(core != turn)
        def _():
            send_to(i, mate)

        return 0

    def keep_chunk(i, _):
        recv[i, me] = big[pl.ds(me * LAT + i, ROWS_IN, stride=LATS), :].astype(BF16)
        return 0

    lax.fori_loop(0, LAT, functools.partial(send_chunk, turn=0), 0)

    lax.fori_loop(0, LAT, functools.partial(send_chunk, turn=1), 0)

    lax.fori_loop(0, LAT, keep_chunk, 0)

    for weight in weights:
        weight.start()

    def place(level, carry):
        slab, slot = carry
        rowoff[level] = jnp.minimum(slab, LEVD - 1) * ROWS_IN + jnp.minimum(slot, SLOTS - 1) * LON
        more = slot + 1
        ends = more >= counts_ref[jnp.minimum(slab, LEVD - 1)]
        return jnp.where(ends, slab + 1, slab), jnp.where(ends, 0, more)

    lax.fori_loop(0, LEV, place, (jnp.int32(0), jnp.int32(0)))

    def begin(slab, start):
        starts[slab] = jnp.minimum(start, LEV - 1)
        return start + counts_ref[slab]

    lax.fori_loop(0, LEVD, begin, jnp.int32(0))

    def shift_rows(level, _):
        srow[pl.ds(level, 1), :] = jnp.full((1, C), shifts_ref[level // 2], jnp.int32)
        return 0

    lax.fori_loop(0, LEV, shift_rows, 0)

    row = lax.broadcasted_iota(jnp.int32, (2 * BAND, C), 0)

    def own_rows(p, _):
        shift = jnp.where(row < BAND, shifts_ref[2 * p], shifts_ref[2 * p + 1])
        for half in range(2):
            own = (lax.rem(row, HALF) + half * HALF >= shift) == (shift <= HALF)
            mask[half, pl.ds(pl.multiple_of(p * 2 * BAND, 2 * BAND), 2 * BAND), :] = own.astype(jnp.int32)
        return 0

    lax.fori_loop(0, BANDS // 2, own_rows, 0)

    def halo_copy(i, half, side):
        return pltpu.make_async_remote_copy(
            src_ref=hsend.at[i, half], dst_ref=hrecv.at[i, half],
            send_sem=h_send.at[i, half], recv_sem=h_recv.at[i, half],
            device_id={"lon": side}, device_id_type=MESH,
        )

    def column_at(i, half, n):
        return (half * SUBS + i // 2) * PROWS + lax.rem(i, 2) * HALF + n

    masks64 = head_masks(LEV)
    ones64 = jnp.concatenate([m.astype(BF16) for m in masks64], 0)

    def column_chunk(i, _):
        pltpu.make_async_copy(
            recv.at[i, pl.ds(0, LEVD - 1)], recv.at[i, pl.ds(0, LEVD - 1)], in_recv.at[i]
        ).wait()

        def widen_in(d, _):
            r32[pl.ds(pl.multiple_of(d * ROWS_IN, ROWS_IN), ROWS_IN), :] = recv[i, d].astype(F32)
            return 0

        lax.fori_loop(0, LEVD, widen_in, 0, unroll=4)

        def pick(level, _):
            xl[pl.ds(pl.multiple_of(level * 16, 16), 16), :] = r32[pl.ds(rowoff[level], 16), :]
            return 0

        lax.fori_loop(0, LEV, pick, 0, unroll=16)

        cols = jnp.concatenate([xl[pl.ds(lon, LEV, stride=16), :] for lon in range(LON)], 0)
        packed = dot(norm(cols, gcol_ref[...]), wcq_ref[...]).astype(BF16)
        parts = []
        for n in range(LON):
            one = packed[n * LEV:(n + 1) * LEV]
            parts.append(attend_short(one[:, :C], one[:, C:2 * C], one[:, 2 * C:], masks64, ones64))
        done = cols + dot(jnp.concatenate(parts, 0).astype(BF16), wco_ref[...])
        normed = norm(done, gwin_ref[...])
        for half in range(2):
            for n in range(HALF):
                part = slice((half * HALF + n) * LEV, (half * HALF + n + 1) * LEV)
                after[pl.ds(column_at(i, half, n), LEV, stride=PART), :] = done[part]
                hsend[i, half, pl.ds(n * LEV, LEV), :] = normed[part]
            halo_copy(i, half, west if half == 0 else east).start()
        return 0

    def merge_chunk(i, _):
        for half in range(2):
            halo_copy(i, half, west if half == 0 else east).wait_recv()
            for n in range(HALF):
                lon = half * HALF + n
                shift = srow[...]
                own = (lon >= shift) == (shift <= HALF)
                mine = hsend[i, half, pl.ds(n * LEV, LEV), :].astype(F32)
                other = hrecv[i, half, pl.ds(n * LEV, LEV), :].astype(F32)
                wtok[pl.ds(column_at(i, half, n), LEV, stride=PART), :] = jnp.where(own, mine, other)
        return 0

    for weight in weights:
        weight.wait()
    lax.fori_loop(0, LAT, column_chunk, 0)
    lax.fori_loop(0, LAT, merge_chunk, 0)

    extra = SEQ - C
    masks128 = head_masks(C)
    ones128 = [m.astype(BF16) for m in masks128]
    ones_pairs = [jnp.concatenate(ones128[h:h + 2], 0) for h in (0, 2)]
    tail_ones = jnp.concatenate(
        [m[:extra] for m in ones128] + [jnp.zeros((C - HEADS * extra, C), BF16)], 0
    )
    tail_lane = lax.broadcasted_iota(jnp.int32, (SEQ, C), 1) // extra
    tail_masks = [tail_lane == h for h in range(HEADS)]

    def back_copy(g, half, side):
        parts = pl.ds(half * SUBS, SUBS)
        rows = pl.ds(pl.multiple_of(g * GROWS, GROWS), GROWS)
        return pltpu.make_async_remote_copy(
            src_ref=attd.at[parts, rows], dst_ref=back.at[parts, rows],
            send_sem=b_send.at[half, g], recv_sem=b_recv.at[half, g],
            device_id={"lon": side}, device_id_type=MESH,
        )

    def window_group(g, _):
        at = pl.multiple_of(g * GROWS, GROWS)
        pieces = []
        for band in range(GROUP):
            for part in range(PARTS):
                pieces.append(wtok[pl.ds(part * PROWS + at + band * BAND, BAND), :])
        tokens = jnp.concatenate(pieces, 0).astype(BF16)
        packed = dot(tokens, wwq_ref[...]).astype(BF16)
        bands = []
        for band in range(GROUP):
            one = packed[band * SEQ:(band + 1) * SEQ]
            bands.append(attend_long(
                one[:, :C], one[:, C:2 * C], one[:, 2 * C:], masks128, tail_masks, ones_pairs, tail_ones
            ))
        for part in range(PARTS):
            rows = slice(part * BAND, (part + 1) * BAND)
            attd[part, pl.ds(at, GROWS), :] = jnp.concatenate([b[rows] for b in bands], 0).astype(BF16)
        back_copy(g, 0, east).start()
        back_copy(g, 1, west).start()
        return 0

    lax.fori_loop(0, GROUPS, window_group, 0)

    def out_copy(part, dest):
        return pltpu.make_async_remote_copy(
            src_ref=msg.at[part, dest], dst_ref=got.at[part, me],
            send_sem=o_send.at[part], recv_sem=o_recv.at[part],
            device_id={"lev": dest}, device_id_type=MESH,
        )

    def feed_part(part, _):
        half = part // SUBS
        attended = jnp.where(
            mask[half] > 0, attd[part].astype(F32), back[part].astype(F32)
        ).astype(BF16)
        stay = after[pl.ds(pl.multiple_of(part * PROWS, PROWS), PROWS), :] + dot(attended, wwo_ref[...])
        hidden = gelu(dot(norm(stay, gmlp_ref[...]), wup_ref[...]))
        blk[pl.ds(0, PROWS), :] = stay + dot(hidden.astype(BF16), wdn_ref[...])

        def fill(dest, _):
            rows = blk[pl.ds(starts[dest] * PART, ROWS_OUT), :]
            msg[part, dest] = jnp.where(row < counts_ref[dest] * PART, rows, 0.0).astype(BF16)
            return 0

        lax.fori_loop(0, LEVD, fill, 0)
        for dy, dx in CHIPS[:-1]:
            for turn in range(2):
                out_copy(part, chip_at(me, dy, dx) + turn).start()
        out_copy(part, mate).start()
        got[part, me] = msg[part, me]
        return 0

    blk[pl.ds(PROWS, ROWS_OUT), :] = jnp.zeros((ROWS_OUT, C), F32)
    for half in range(2):
        for g in range(GROUPS):
            back_copy(g, half, east if half == 0 else west).wait_recv()
        lax.fori_loop(half * SUBS, (half + 1) * SUBS, feed_part, 0)

    stage = LEVD * ROWS_OUT

    def take_part(part, _):
        pltpu.make_async_copy(
            got.at[part, pl.ds(0, LEVD - 1)], got.at[part, pl.ds(0, LEVD - 1)], o_recv.at[part]
        ).wait()

        def widen_out(e, _):
            big[pl.ds(pl.multiple_of(e * ROWS_OUT, ROWS_OUT), ROWS_OUT), :] = got[part, e].astype(F32)
            return 0

        lax.fori_loop(0, LEVD, widen_out, 0, unroll=4)

        def sort(n, _):
            slot, lon = n // HALF, lax.rem(n, HALF)
            for i in range(2):
                big[pl.ds(stage + n * LATS + lax.rem(part, SUBS) * 2 + i, LEVD, stride=LAT), :] = big[
                    pl.ds(slot * PART + i * HALF + lon, LEVD, stride=ROWS_OUT), :
                ]
            return 0

        lax.fori_loop(0, SLOTS * HALF, sort, 0, unroll=4)
        return 0

    for half in range(2):
        lax.fori_loop(half * SUBS, (half + 1) * SUBS, take_part, 0)

        def give(n, _):
            slot, lon = n // HALF, lax.rem(n, HALF)
            rows = big[pl.ds(pl.multiple_of(stage + n * LATS, LATS), LATS), :]
            out_ref[slot * LON + half * HALF + lon] = rows.astype(BF16)
            return 0

        lax.fori_loop(0, SLOTS * HALF, give, 0, unroll=4)

    for i in range(LAT):
        pltpu.make_async_copy(
            sendbuf.at[i, pl.ds(0, LEVD - 1)], sendbuf.at[i, pl.ds(0, LEVD - 1)], in_send.at[i]
        ).wait()
        halo_copy(i, 0, west).wait_send()
        halo_copy(i, 1, east).wait_send()
    for g in range(GROUPS):
        back_copy(g, 0, east).wait_send()
        back_copy(g, 1, west).wait_send()
    for part in range(PARTS):
        pltpu.make_async_copy(
            msg.at[part, pl.ds(0, LEVD - 1)], msg.at[part, pl.ds(0, LEVD - 1)], o_send.at[part]
        ).wait()


def per_device(
    levels_in, slab_levels, shifts, gain_col, w_col_qkv, w_col_out, gain_win, w_win_qkv, w_win_out,
    gain_mlp, w_up, w_down,
):
    x = levels_in.transpose(0, 2, 1, 3).reshape(ROWS_IN, LATS, C)
    weights = [
        gain_col.reshape(1, C), w_col_qkv, w_col_out, gain_win.reshape(1, C), w_win_qkv, w_win_out,
        gain_mlp.reshape(1, C), w_up, w_down,
    ]
    smem = pl.BlockSpec(memory_space=pltpu.SMEM)
    vmem = pl.BlockSpec(memory_space=pltpu.VMEM)
    dma = pltpu.SemaphoreType.DMA
    out = pl.pallas_call(
        kernel,
        out_shape=pltpu.VMEM((ROWS_IN, LATS, C), BF16),
        in_specs=[smem, smem] + [pl.BlockSpec(memory_space=pl.ANY)] * 10,
        out_specs=vmem,
        scratch_shapes=[
            *[pltpu.VMEM(w.shape, w.dtype) for w in weights],
            pltpu.SMEM((LEV,), jnp.int32),
            pltpu.SMEM((LEVD,), jnp.int32),
            pltpu.VMEM((ROWS_IN, LATS, C), BF16),
            pltpu.VMEM((ROWS_IN * LATS, C), F32),
            pltpu.VMEM((LAT, LEVD, ROWS_IN, C), BF16),
            pltpu.VMEM((LAT, LEVD, ROWS_IN, C), BF16),
            pltpu.VMEM((LEVD * ROWS_IN + 8, C), F32),
            pltpu.VMEM((LEV * 16, C), F32),
            pltpu.VMEM((LEV, C), jnp.int32),
            pltpu.VMEM((PARTS * PROWS, C), F32),
            pltpu.VMEM((LAT, 2, HCOL, C), BF16),
            pltpu.VMEM((LAT, 2, HCOL, C), BF16),
            pltpu.VMEM((PARTS * PROWS, C), F32),
            pltpu.VMEM((PARTS, PROWS, C), BF16),
            pltpu.VMEM((PARTS, PROWS, C), BF16),
            pltpu.VMEM((2, PROWS, C), jnp.int32),
            pltpu.VMEM((PROWS + ROWS_OUT, C), F32),
            pltpu.VMEM((PARTS, LEVD, ROWS_OUT, C), BF16),
            pltpu.VMEM((PARTS, LEVD, ROWS_OUT, C), BF16),
            dma((SLOTS,)), dma((9,)),
            dma((LAT,)), dma((LAT,)),
            dma((LAT, 2)), dma((LAT, 2)),
            dma((2, GROUPS)), dma((2, GROUPS)),
            dma((PARTS,)), dma((PARTS,)),
        ],
        compiler_params=pltpu.CompilerParams(
            collective_id=0, has_side_effects=True, vmem_limit_bytes=56 * 1024 * 1024
        ),
    )(slab_levels, shifts, x, *weights)
    return out.reshape(SLOTS, LON, LATS, C).transpose(0, 2, 1, 3)


def solution(mesh):
    placed = (P("lev", None, "lon", None),) + (P(),) * 11
    return jax.shard_map(
        per_device,
        mesh=mesh,
        in_specs=placed,
        out_specs=P("lev", None, "lon", None),
        check_vma=False,
    )
```

```python
import functools
import math

import jax
import jax.numpy as jnp
from jax import lax
from jax.experimental import pallas as pl
from jax.experimental.pallas import tpu as pltpu
from jax.sharding import PartitionSpec as P

HEADS = 4
EPS = 1e-05
MESH = pl.DeviceIdType.MESH
F32 = jnp.float32
BF16 = jnp.bfloat16

SLOTS = 4
LON = 12
LAT = 6
HALF = LON // 2
LEVD = 32
LEV = 64
LATS = LAT * LEVD
C = 128
SUBS = 3
PART = HALF * LAT // SUBS
PARTS = 2 * SUBS
ROWS_IN = SLOTS * LON
ROWS_OUT = SLOTS * PART
PROWS = LEV * PART
BAND = 2 * PART
SEQ = PARTS * BAND
BANDS = LEV // 2
GROUPS = 8
GROUP = BANDS // GROUPS
GROWS = GROUP * BAND
HCOL = HALF * LEV
GELU_A = math.sqrt(2.0 / math.pi)
GELU_B = GELU_A * 0.044715
SCALE = math.log2(math.e) / math.sqrt(C // HEADS)


def norm(v, gain):
    centred = v - jnp.mean(v, -1, keepdims=True)
    spread = jnp.mean(centred * centred, -1, keepdims=True)
    return (centred * lax.rsqrt(spread + EPS) * gain).astype(BF16)


def dot(a, b):
    return jnp.dot(a, b, preferred_element_type=F32)


def dot_nt(a, b):
    return lax.dot_general(a, b, (((1,), (1,)), ((), ())), preferred_element_type=F32)


def head_masks(rows):
    lane = lax.broadcasted_iota(jnp.int32, (rows, C), 1)
    return [(lane // (C // HEADS)) == h for h in range(HEADS)]


def attend_short(q, k, v, masks, ones):
    zero = jnp.zeros_like(k)
    keys = jnp.concatenate([jnp.where(m, k, zero) for m in masks], 0)
    values = jnp.concatenate([jnp.where(m, v, zero) for m in masks], 0)
    scores = dot_nt(q, keys)
    low = lax.broadcasted_iota(jnp.int32, (LEV, C), 1) < LEV
    probs = []
    for t in range(2):
        part = scores[:, t * C:(t + 1) * C]
        top = jnp.where(
            low,
            jnp.max(jnp.where(low, part, -jnp.inf), -1, keepdims=True),
            jnp.max(jnp.where(low, -jnp.inf, part), -1, keepdims=True),
        )
        probs.append(jnp.exp2((part - top) * SCALE).astype(BF16))
    both = dot(jnp.concatenate(probs, 1), jnp.concatenate([values, ones], 1))
    return both[:, :C] / both[:, C:]


def attend_long(q, k, v, masks, tail_masks, ones, tail_ones):
    extra = SEQ - C
    tail_of = [m[:extra] for m in masks]
    km, kt, vm, vt = k[:C], k[C:], v[:C], v[C:]
    zero, none = jnp.zeros_like(km), jnp.zeros_like(kt)
    pad = jnp.zeros((C - HEADS * extra, C), BF16)
    tail = dot_nt(q, jnp.concatenate([jnp.where(m, kt, none) for m in tail_of] + [pad], 0))
    tops, total = jnp.zeros((SEQ, C), F32), None
    for first in range(0, HEADS, 2):
        heads = (first, first + 1)
        scores = dot_nt(q, jnp.concatenate([jnp.where(masks[h], km, zero) for h in heads], 0))
        probs = []
        for n, h in enumerate(heads):
            mine = scores[:, n * C:(n + 1) * C]
            top = jnp.max(jnp.maximum(mine, jnp.where(tail_masks[h], tail, -jnp.inf)), -1, keepdims=True)
            probs.append(jnp.exp2((mine - top) * SCALE).astype(BF16))
            tops = jnp.where(tail_masks[h], top, tops)
        values = jnp.concatenate([jnp.where(masks[h], vm, zero) for h in heads], 0)
        part = dot(jnp.concatenate(probs, 1), jnp.concatenate([values, ones[first // 2]], 1))
        total = part if total is None else total + part
    probs = jnp.exp2((tail - tops) * SCALE).astype(BF16)
    values = jnp.concatenate([jnp.where(m, vt, none) for m in tail_of] + [pad], 0)
    total = total + dot(probs, jnp.concatenate([values, tail_ones], 1))
    return total[:, :C] / total[:, C:]


def gelu(v):
    inner = v * (GELU_A + GELU_B * (v * v))
    half = 0.5 * v
    return half * jnp.tanh(inner) + half


CHIPS = (
    (2, 2), (2, 1), (1, 2), (2, 3), (3, 2), (1, 1), (3, 3), (1, 3), (3, 1), (2, 0), (0, 2),
    (0, 1), (0, 3), (1, 0), (3, 0), (0, 0),
)


def chip_at(me, dy, dx):
    x, y = lax.rem(me // 2, 4), me // 8
    return (lax.rem(y + dy, 4) * 4 + lax.rem(x + dx, 4)) * 2


def kernel(
    counts_ref, shifts_ref, x_ref, gcol_hbm, wcq_hbm, wco_hbm, gwin_hbm, wwq_hbm, wwo_hbm,
    gmlp_hbm, wup_hbm, wdn_hbm, out_ref,
    gcol_ref, wcq_ref, wco_ref, gwin_ref, wwq_ref, wwo_ref, gmlp_ref, wup_ref, wdn_ref,
    rowoff, starts, xin, big, sendbuf, recv, r32, xl, srow, after, hsend, hrecv, wtok, attd, back,
    mask, blk, msg, got,
    x_sem, w_sem, in_send, in_recv, h_send, h_recv, b_send, b_recv, o_send, o_recv,
):
    me = lax.axis_index("lev")
    z = lax.axis_index("lon")
    east = lax.rem(z + 1, 8)
    west = lax.rem(z + 7, 8)

    barrier = pltpu.get_barrier_semaphore()

    def x_copy(slot):
        part = pl.ds(slot * LON, LON)
        return pltpu.make_async_copy(x_ref.at[part], xin.at[part], x_sem.at[slot])

    for slot in range(SLOTS):
        x_copy(slot).start()
    weights = [
        pltpu.make_async_copy(far, near, w_sem.at[n])
        for n, (far, near) in enumerate([
            (gcol_hbm, gcol_ref), (wcq_hbm, wcq_ref), (wco_hbm, wco_ref), (gwin_hbm, gwin_ref),
            (wwq_hbm, wwq_ref), (wwo_hbm, wwo_ref), (gmlp_hbm, gmlp_ref), (wup_hbm, wup_ref),
            (wdn_hbm, wdn_ref),
        ])
    ]

    def greet(step, _):
        pl.semaphore_signal(barrier, inc=1, device_id={"lev": lax.rem(me + step, LEVD)}, device_id_type=MESH)
        return 0

    lax.fori_loop(1, LEVD, greet, 0)
    for side in (east, west):
        pl.semaphore_signal(barrier, inc=1, device_id={"lon": side}, device_id_type=MESH)

    def widen(n, _):
        big[pl.ds(pl.multiple_of(n * LATS, LATS), LATS), :] = xin[n].astype(F32)
        return 0

    for slot in range(SLOTS):
        x_copy(slot).wait()
        lax.fori_loop(slot * LON, (slot + 1) * LON, widen, 0)
    pl.semaphore_wait(barrier, LEVD - 1 + 2)

    def in_copy(i, dest):
        return pltpu.make_async_remote_copy(
            src_ref=sendbuf.at[i, dest], dst_ref=recv.at[i, me],
            send_sem=in_send.at[i], recv_sem=in_recv.at[i],
            device_id={"lev": dest}, device_id_type=MESH,
        )

    core = lax.rem(me, 2)
    mate = me + 1 - 2 * core

    def send_to(i, dest):
        sendbuf[i, dest] = big[pl.ds(dest * LAT + i, ROWS_IN, stride=LATS), :].astype(BF16)
        in_copy(i, dest).start()

    def send_chunk(i, _, turn):
        for dy, dx in CHIPS[:-1]:
            send_to(i, chip_at(me, dy, dx) + turn)

        @pl.when(core != turn)
        def _():
            send_to(i, mate)

        return 0

    def keep_chunk(i, _):
        recv[i, me] = big[pl.ds(me * LAT + i, ROWS_IN, stride=LATS), :].astype(BF16)
        return 0

    lax.fori_loop(0, LAT, functools.partial(send_chunk, turn=0), 0)

    lax.fori_loop(0, LAT, functools.partial(send_chunk, turn=1), 0)

    lax.fori_loop(0, LAT, keep_chunk, 0)

    for weight in weights:
        weight.start()

    def place(level, carry):
        slab, slot = carry
        rowoff[level] = jnp.minimum(slab, LEVD - 1) * ROWS_IN + jnp.minimum(slot, SLOTS - 1) * LON
        more = slot + 1
        ends = more >= counts_ref[jnp.minimum(slab, LEVD - 1)]
        return jnp.where(ends, slab + 1, slab), jnp.where(ends, 0, more)

    lax.fori_loop(0, LEV, place, (jnp.int32(0), jnp.int32(0)))

    def halo_copy(i, half, side):
        return pltpu.make_async_remote_copy(
            src_ref=hsend.at[i, half], dst_ref=hrecv.at[i, half],
            send_sem=h_send.at[i, half], recv_sem=h_recv.at[i, half],
            device_id={"lon": side}, device_id_type=MESH,
        )

    def column_at(i, half, n):
        return (half * SUBS + i // 2) * PROWS + lax.rem(i, 2) * HALF + n

    masks64 = head_masks(LEV)
    ones64 = jnp.concatenate([m.astype(BF16) for m in masks64], 0)

    def column_chunk(i, _):
        pltpu.make_async_copy(
            recv.at[i, pl.ds(0, LEVD - 1)], recv.at[i, pl.ds(0, LEVD - 1)], in_recv.at[i]
        ).wait()

        def widen_in(d, _):
            r32[pl.ds(pl.multiple_of(d * ROWS_IN, ROWS_IN), ROWS_IN), :] = recv[i, d].astype(F32)
            return 0

        lax.fori_loop(0, LEVD, widen_in, 0, unroll=4)

        def pick(level, _):
            xl[pl.ds(pl.multiple_of(level * 16, 16), 16), :] = r32[pl.ds(rowoff[level], 16), :]
            return 0

        lax.fori_loop(0, LEV, pick, 0, unroll=16)

        cols = jnp.concatenate([xl[pl.ds(lon, LEV, stride=16), :] for lon in range(LON)], 0)
        packed = dot(norm(cols, gcol_ref[...]), wcq_ref[...]).astype(BF16)
        parts = []
        for n in range(LON):
            one = packed[n * LEV:(n + 1) * LEV]
            parts.append(attend_short(one[:, :C], one[:, C:2 * C], one[:, 2 * C:], masks64, ones64))
        done = cols + dot(jnp.concatenate(parts, 0).astype(BF16), wco_ref[...])
        normed = norm(done, gwin_ref[...])
        for half in range(2):
            for n in range(HALF):
                part = slice((half * HALF + n) * LEV, (half * HALF + n + 1) * LEV)
                after[pl.ds(column_at(i, half, n), LEV, stride=PART), :] = done[part]
                hsend[i, half, pl.ds(n * LEV, LEV), :] = normed[part]
            halo_copy(i, half, west if half == 0 else east).start()
        return 0

    def merge_chunk(i, _):
        for half in range(2):
            halo_copy(i, half, west if half == 0 else east).wait_recv()
            for n in range(HALF):
                lon = half * HALF + n
                shift = srow[...]
                own = (lon >= shift) == (shift <= HALF)
                mine = hsend[i, half, pl.ds(n * LEV, LEV), :].astype(F32)
                other = hrecv[i, half, pl.ds(n * LEV, LEV), :].astype(F32)
                wtok[pl.ds(column_at(i, half, n), LEV, stride=PART), :] = jnp.where(own, mine, other)
        return 0

    for weight in weights:
        weight.wait()
    lax.fori_loop(0, LAT, column_chunk, 0)
    def begin(slab, start):
        starts[slab] = jnp.minimum(start, LEV - 1)
        return start + counts_ref[slab]

    lax.fori_loop(0, LEVD, begin, jnp.int32(0))

    def shift_rows(level, _):
        srow[pl.ds(level, 1), :] = jnp.full((1, C), shifts_ref[level // 2], jnp.int32)
        return 0

    lax.fori_loop(0, LEV, shift_rows, 0)

    row = lax.broadcasted_iota(jnp.int32, (2 * BAND, C), 0)

    def own_rows(p, _):
        shift = jnp.where(row < BAND, shifts_ref[2 * p], shifts_ref[2 * p + 1])
        for half in range(2):
            own = (lax.rem(row, HALF) + half * HALF >= shift) == (shift <= HALF)
            mask[half, pl.ds(pl.multiple_of(p * 2 * BAND, 2 * BAND), 2 * BAND), :] = own.astype(jnp.int32)
        return 0

    lax.fori_loop(0, BANDS // 2, own_rows, 0)

    lax.fori_loop(0, LAT, merge_chunk, 0)

    extra = SEQ - C
    masks128 = head_masks(C)
    ones128 = [m.astype(BF16) for m in masks128]
    ones_pairs = [jnp.concatenate(ones128[h:h + 2], 0) for h in (0, 2)]
    tail_ones = jnp.concatenate(
        [m[:extra] for m in ones128] + [jnp.zeros((C - HEADS * extra, C), BF16)], 0
    )
    tail_lane = lax.broadcasted_iota(jnp.int32, (SEQ, C), 1) // extra
    tail_masks = [tail_lane == h for h in range(HEADS)]

    def back_copy(g, half, side):
        parts = pl.ds(half * SUBS, SUBS)
        rows = pl.ds(pl.multiple_of(g * GROWS, GROWS), GROWS)
        return pltpu.make_async_remote_copy(
            src_ref=attd.at[parts, rows], dst_ref=back.at[parts, rows],
            send_sem=b_send.at[half, g], recv_sem=b_recv.at[half, g],
            device_id={"lon": side}, device_id_type=MESH,
        )

    def window_group(g, _):
        at = pl.multiple_of(g * GROWS, GROWS)
        pieces = []
        for band in range(GROUP):
            for part in range(PARTS):
                pieces.append(wtok[pl.ds(part * PROWS + at + band * BAND, BAND), :])
        tokens = jnp.concatenate(pieces, 0).astype(BF16)
        packed = dot(tokens, wwq_ref[...]).astype(BF16)
        bands = []
        for band in range(GROUP):
            one = packed[band * SEQ:(band + 1) * SEQ]
            bands.append(attend_long(
                one[:, :C], one[:, C:2 * C], one[:, 2 * C:], masks128, tail_masks, ones_pairs, tail_ones
            ))
        for part in range(PARTS):
            rows = slice(part * BAND, (part + 1) * BAND)
            attd[part, pl.ds(at, GROWS), :] = jnp.concatenate([b[rows] for b in bands], 0).astype(BF16)
        back_copy(g, 0, east).start()
        back_copy(g, 1, west).start()
        return 0

    lax.fori_loop(0, GROUPS, window_group, 0)

    def out_copy(part, dest):
        return pltpu.make_async_remote_copy(
            src_ref=msg.at[part, dest], dst_ref=got.at[part, me],
            send_sem=o_send.at[part], recv_sem=o_recv.at[part],
            device_id={"lev": dest}, device_id_type=MESH,
        )

    def feed_part(part, _):
        half = part // SUBS
        attended = jnp.where(
            mask[half] > 0, attd[part].astype(F32), back[part].astype(F32)
        ).astype(BF16)
        stay = after[pl.ds(pl.multiple_of(part * PROWS, PROWS), PROWS), :] + dot(attended, wwo_ref[...])
        hidden = gelu(dot(norm(stay, gmlp_ref[...]), wup_ref[...]))
        blk[pl.ds(0, PROWS), :] = stay + dot(hidden.astype(BF16), wdn_ref[...])

        def fill(dest, _):
            rows = blk[pl.ds(starts[dest] * PART, ROWS_OUT), :]
            msg[part, dest] = jnp.where(row < counts_ref[dest] * PART, rows, 0.0).astype(BF16)
            return 0

        lax.fori_loop(0, LEVD, fill, 0)
        for dy, dx in CHIPS[:-1]:
            for turn in range(2):
                out_copy(part, chip_at(me, dy, dx) + turn).start()
        out_copy(part, mate).start()
        got[part, me] = msg[part, me]
        return 0

    blk[pl.ds(PROWS, ROWS_OUT), :] = jnp.zeros((ROWS_OUT, C), F32)
    for half in range(2):
        for g in range(GROUPS):
            back_copy(g, half, east if half == 0 else west).wait_recv()
        lax.fori_loop(half * SUBS, (half + 1) * SUBS, feed_part, 0)

    stage = LEVD * ROWS_OUT

    def take_part(part, _):
        pltpu.make_async_copy(
            got.at[part, pl.ds(0, LEVD - 1)], got.at[part, pl.ds(0, LEVD - 1)], o_recv.at[part]
        ).wait()

        def widen_out(e, _):
            big[pl.ds(pl.multiple_of(e * ROWS_OUT, ROWS_OUT), ROWS_OUT), :] = got[part, e].astype(F32)
            return 0

        lax.fori_loop(0, LEVD, widen_out, 0, unroll=4)

        def sort(n, _):
            slot, lon = n // HALF, lax.rem(n, HALF)
            for i in range(2):
                big[pl.ds(stage + n * LATS + lax.rem(part, SUBS) * 2 + i, LEVD, stride=LAT), :] = big[
                    pl.ds(slot * PART + i * HALF + lon, LEVD, stride=ROWS_OUT), :
                ]
            return 0

        lax.fori_loop(0, SLOTS * HALF, sort, 0, unroll=4)
        return 0

    for half in range(2):
        lax.fori_loop(half * SUBS, (half + 1) * SUBS, take_part, 0)

        def give(n, _):
            slot, lon = n // HALF, lax.rem(n, HALF)
            rows = big[pl.ds(pl.multiple_of(stage + n * LATS, LATS), LATS), :]
            out_ref[slot * LON + half * HALF + lon] = rows.astype(BF16)
            return 0

        lax.fori_loop(0, SLOTS * HALF, give, 0, unroll=4)

    for i in range(LAT):
        pltpu.make_async_copy(
            sendbuf.at[i, pl.ds(0, LEVD - 1)], sendbuf.at[i, pl.ds(0, LEVD - 1)], in_send.at[i]
        ).wait()
        halo_copy(i, 0, west).wait_send()
        halo_copy(i, 1, east).wait_send()
    for g in range(GROUPS):
        back_copy(g, 0, east).wait_send()
        back_copy(g, 1, west).wait_send()
    for part in range(PARTS):
        pltpu.make_async_copy(
            msg.at[part, pl.ds(0, LEVD - 1)], msg.at[part, pl.ds(0, LEVD - 1)], o_send.at[part]
        ).wait()


def per_device(
    levels_in, slab_levels, shifts, gain_col, w_col_qkv, w_col_out, gain_win, w_win_qkv, w_win_out,
    gain_mlp, w_up, w_down,
):
    x = levels_in.transpose(0, 2, 1, 3).reshape(ROWS_IN, LATS, C)
    weights = [
        gain_col.reshape(1, C), w_col_qkv, w_col_out, gain_win.reshape(1, C), w_win_qkv, w_win_out,
        gain_mlp.reshape(1, C), w_up, w_down,
    ]
    smem = pl.BlockSpec(memory_space=pltpu.SMEM)
    vmem = pl.BlockSpec(memory_space=pltpu.VMEM)
    dma = pltpu.SemaphoreType.DMA
    out = pl.pallas_call(
        kernel,
        out_shape=pltpu.VMEM((ROWS_IN, LATS, C), BF16),
        in_specs=[smem, smem] + [pl.BlockSpec(memory_space=pl.ANY)] * 10,
        out_specs=vmem,
        scratch_shapes=[
            *[pltpu.VMEM(w.shape, w.dtype) for w in weights],
            pltpu.SMEM((LEV,), jnp.int32),
            pltpu.SMEM((LEVD,), jnp.int32),
            pltpu.VMEM((ROWS_IN, LATS, C), BF16),
            pltpu.VMEM((ROWS_IN * LATS, C), F32),
            pltpu.VMEM((LAT, LEVD, ROWS_IN, C), BF16),
            pltpu.VMEM((LAT, LEVD, ROWS_IN, C), BF16),
            pltpu.VMEM((LEVD * ROWS_IN + 8, C), F32),
            pltpu.VMEM((LEV * 16, C), F32),
            pltpu.VMEM((LEV, C), jnp.int32),
            pltpu.VMEM((PARTS * PROWS, C), F32),
            pltpu.VMEM((LAT, 2, HCOL, C), BF16),
            pltpu.VMEM((LAT, 2, HCOL, C), BF16),
            pltpu.VMEM((PARTS * PROWS, C), F32),
            pltpu.VMEM((PARTS, PROWS, C), BF16),
            pltpu.VMEM((PARTS, PROWS, C), BF16),
            pltpu.VMEM((2, PROWS, C), jnp.int32),
            pltpu.VMEM((PROWS + ROWS_OUT, C), F32),
            pltpu.VMEM((PARTS, LEVD, ROWS_OUT, C), BF16),
            pltpu.VMEM((PARTS, LEVD, ROWS_OUT, C), BF16),
            dma((SLOTS,)), dma((9,)),
            dma((LAT,)), dma((LAT,)),
            dma((LAT, 2)), dma((LAT, 2)),
            dma((2, GROUPS)), dma((2, GROUPS)),
            dma((PARTS,)), dma((PARTS,)),
        ],
        compiler_params=pltpu.CompilerParams(
            collective_id=0, has_side_effects=True, vmem_limit_bytes=56 * 1024 * 1024
        ),
    )(slab_levels, shifts, x, *weights)
    return out.reshape(SLOTS, LON, LATS, C).transpose(0, 2, 1, 3)


def solution(mesh):
    placed = (P("lev", None, "lon", None),) + (P(),) * 11
    return jax.shard_map(
        per_device,
        mesh=mesh,
        in_specs=placed,
        out_specs=P("lev", None, "lon", None),
        check_vma=False,
    )
```
